256 devices in a mesh: ctx: 64 (over y, z, core), ch: 4 (over x).
Axes of the slice: x: 4, y: 4, z: 8, core: 2. Of those that a mesh axis runs over, the one named last changes fastest.
Arguments:
- q_in: bfloat16 [8192, 4096], P('ctx', 'ch'), may hold values from -6 to 6
- k_in: bfloat16 [8192, 4096], P('ctx', 'ch'), may hold values from -6 to 6
- v_in: bfloat16 [8192, 4096], P('ctx', 'ch'), may hold values from -6 to 6
- short_taps: float32 [3, 3, 4096], P(None, None, 'ch'), may hold values from -3 to 3
- skip_bias: float32 [4096], P('ch'), may hold values from -4.5 to 4.5
- norm_gain: float32 [4096], P('ch'), may hold values from 0.1 to 1.9
- filter_spectrum: float32 [2, 64, 2, 128, 4096], P(None, 'ctx', None, None, 'ch'), may hold values from -6 to 6
Outputs:
- mixer_out: bfloat16 [8192, 4096], P('ctx', 'ch')
The draws below stay inside these ranges and needn't reach their ends.
All inputs are finite; a program needn't handle non-finite values.
Results may differ from the reference program's by a relative error of at most 0.001.
Values may be sent and summed in bfloat16 or wider, within the bound.
A program may use at most 64 MiB of HBM per device.

```python
import math
import jax
import jax.numpy as jnp
import numpy as np
from jax import lax

LOC = 128
C = 4096
KS = 3
TOKENS = 8192
BLOCKS = 128
FFT_LEN = 16384
N_CTX = 64


def draw_skip_bias(key, part):
    key = jax.random.fold_in(key, 11)
    first, second = jax.random.split(key)
    ramp = 1.0 + 2.0 * jnp.arange(C, dtype=jnp.float32) / (C - 1)
    signs = jnp.where(jax.random.uniform(first, (C,)) < 0.5, -1.0, 1.0)
    spread = jax.random.uniform(second, (C,), minval=0.5, maxval=1.4)
    return (signs * ramp * spread).astype(jnp.float32)


def block_levels(own_key, extent, cuts, low, top_value):
    loudness = 1.0
    for position, blocks in cuts:
        heights = jax.random.uniform(jax.random.fold_in(jax.random.fold_in(own_key, 6), position), (blocks,), jnp.float32, low / len(cuts), top_value / len(cuts))
        loudness = loudness * jnp.repeat(jnp.exp(heights), extent[position] // blocks).reshape((-1,) + (1,) * (len(extent) - 1 - position))
    return loudness


def bell_draw(stream_key, extent, scale, most, pieces=(), kind=jnp.bfloat16):
    entries = scale * jax.random.normal(stream_key, extent, jnp.float32)
    if pieces:
        entries = entries * block_levels(stream_key, extent, pieces, -0.22, 0.18)
    return jnp.clip(entries, -most, most).astype(kind)


def setup_inputs(seed: int = 0) -> dict:
    seeds = jax.random.split(jax.random.key(seed), 8)
    return {
        "q_in": bell_draw(seeds[0], (TOKENS, C), 1.0, 6.0, ((0, 64), (1, 4))),
        "k_in": bell_draw(seeds[1], (TOKENS, C), 1.0, 6.0, ((0, 64), (1, 4))),
        "v_in": bell_draw(seeds[2], (TOKENS, C), 1.0, 6.0, ((0, 64), (1, 4))),
        "short_taps": bell_draw(seeds[3], (3, KS, C), 0.6, 3.0, ((2, 4),), jnp.float32),
        "skip_bias": draw_skip_bias(jax.random.fold_in(seeds[7], 71), 0),
        "norm_gain": jnp.clip(1.0 + 0.18 * jax.random.normal(seeds[5], (C,), jnp.float32), 0.1, 1.9),
        "filter_spectrum": bell_draw(seeds[6], (2, N_CTX, 2, LOC, C), 1.0, 6.0, ((1, 64), (4, 4)), jnp.float32),
    }


norm_eps = 1e-06

def reversed_order(devices):
    levels = devices.bit_length() - 1
    positions = np.arange(devices)
    result = np.zeros(devices, np.int64)
    for bit_pos in range(levels):
        result = result + (positions >> bit_pos & 1) * (1 << levels - 1 - bit_pos)
    return result.astype(np.int32)

def short_mix(signal, weights):
    tok_count = signal.shape[0]
    padded = jnp.pad(signal.astype(jnp.float32), ((KS - 1, 0), (0, 0)))
    result = jnp.zeros(signal.shape, jnp.float32)
    for lag_step in range(KS):
        begin = KS - 1 - lag_step
        result = result + weights[lag_step] * padded[begin:begin + tok_count]
    return result

def reference(q_in, k_in, v_in, short_taps, skip_bias, norm_gain, filter_spectrum):
    query = short_mix(q_in, short_taps[0])
    keys = short_mix(k_in, short_taps[1])
    values = short_mix(v_in, short_taps[2])
    mixed = keys * values
    order_table = reversed_order(N_CTX)
    natural = filter_spectrum[:, order_table]
    natural = natural.reshape(2, BLOCKS, LOC, C).transpose(0, 2, 1, 3).reshape(2, FFT_LEN, C)
    group_cols = math.gcd(C, 256)
    groups = C // group_cols
    signal_groups = mixed.reshape(TOKENS, groups, group_cols).transpose(1, 0, 2)
    spec_groups = natural.reshape(2, FFT_LEN, groups, group_cols).transpose(2, 0, 1, 3)

    def convolve(operands):
        signal, spec = operands
        padded = jnp.pad(signal, ((0, FFT_LEN - TOKENS), (0, 0)))
        filtered = jnp.fft.fft(padded, axis=0) * lax.complex(spec[0], spec[1])
        return jnp.real(jnp.fft.ifft(filtered, axis=0))[:TOKENS]
    conv_out = lax.map(convolve, (signal_groups, spec_groups)).transpose(1, 0, 2).reshape(TOKENS, C)
    gated = query * (conv_out + skip_bias * mixed)
    mean_square = lax.optimization_barrier(jnp.mean(gated * gated, axis=1, keepdims=True))
    return (gated * lax.rsqrt(mean_square + norm_eps) * norm_gain).astype(jnp.bfloat16)
```

```python
import functools

import jax
import jax.numpy as jnp
import numpy as np
from jax import lax
from jax.experimental import pallas as pl
from jax.experimental.pallas import tpu as pltpu
from jax.sharding import PartitionSpec as P

MESH = pl.DeviceIdType.MESH
F32 = jnp.float32
BF16 = jnp.bfloat16
EPS = 1e-06
BIAS = 120.0
LN2 = float(np.log(2.0))
IN_MAX = 6.0


class Code:
    def __init__(self, power, top):
        self.power = power
        self.a = (2.0 ** (2.0 * BIAS / power) - 1.0) / top
        self.top = top

    def encode(self, x):
        size = jnp.minimum(jnp.abs(x), self.top)
        size = jnp.exp2((self.power / LN2) * jnp.log(1.0 + self.a * size) - BIAS)
        return jnp.where(x < 0.0, -size, size).astype(BF16)

    def decode(self, code):
        v = code.astype(F32)
        size = jnp.exp2((1.0 / (LN2 * self.power)) * jnp.log(jnp.abs(v)) + BIAS / self.power)
        size = (size - 1.0) * (1.0 / self.a)
        return jnp.where(v < 0.0, -size, size)


FILTER_CODE = Code(30.0, 6.0)
MIXED_CODE = Code(22.0, 1.0)
CONV_CODE = Code(14.0, 768.0)


def split(x):
    high = x.astype(BF16)
    return high, (x - high.astype(F32)).astype(BF16)


def dot3(a, b):
    dot = functools.partial(jnp.dot, preferred_element_type=F32)
    return dot(a[0], b[0]) + (dot(a[0], b[1]) + dot(a[1], b[0]))


def tables(devices, rows):
    levels = devices.bit_length() - 1
    rev = np.array([int(format(e, f"0{levels}b")[::-1], 2) if levels else 0 for e in range(devices)])
    freq = (2 * rev[:, None] + np.arange(2)[None, :]).reshape(-1)
    blocks = 2 * devices
    full = blocks * rows
    turn = 2.0 * np.pi
    ang = turn * ((freq[:, None] * np.arange(devices)[None, :]) % blocks) / blocks
    outer = np.concatenate((np.cos(ang), -np.sin(ang)), 0)
    tw = turn * ((freq[:, None] * np.arange(rows)[None, :]) % full) / full
    ids = np.arange(rows)
    loc = turn * ((ids[:, None] * ids[None, :]) % rows) / rows
    c, s = np.cos(loc), np.sin(loc)
    fwd = np.block([[c, -s], [s, c]])
    inv = np.block([[c, s], [-s, c]])

    def parts(m):
        m = m.astype(np.float32)
        high = m.astype(jnp.bfloat16)
        return np.stack((high, (m - high.astype(np.float32)).astype(jnp.bfloat16)))

    return (
        parts(outer),
        parts(outer.T / full),
        parts(fwd),
        parts(inv),
        np.stack((np.cos(tw), np.sin(tw))).astype(np.float32),
    )


def kernel(
    n, n_ch, channels,
    q_ref, k_ref, v_ref, taps_ref, skip_ref, gain_ref, filt_ref,
    outer_ref, inner_ref, fwd_ref, inv_ref, tw_ref,
    out_ref,
    ext, halo_send, halo_recv, query, mixed, x_send, x_recv, h_send, h_recv, y_send, y_recv,
    work, spec_re, spec_im, sums, sums_recv,
    halo_sems, x_sems, h_sems, y_sems, sum_send, sum_recv,
):
    me, column = lax.axis_index("ctx"), lax.axis_index("ch")
    rows, width = q_ref.shape
    own = width // n
    tiles = width // 128
    per_tile = 128 // own
    ahead = lax.rem(me + 1, n)

    barrier = pltpu.get_barrier_semaphore()

    def greet(i, _):
        pl.semaphore_signal(barrier, inc=1, device_id=(lax.rem(me + i, n), column), device_id_type=MESH)
        return 0

    lax.fori_loop(1, n, greet, 0)
    for i in range(1, n_ch):
        pl.semaphore_signal(barrier, inc=1, device_id=(me, lax.rem(column + i, n_ch)), device_id_type=MESH)

    for i, ref in enumerate((q_ref, k_ref, v_ref)):
        ext[i, 8 : 8 + rows, :] = ref[...].astype(F32)
        halo_send[2 * i : 2 * i + 2, :] = ext[i, 6 + rows : 8 + rows, :]
    halo_send[6:8, :] = jnp.zeros((2, width), F32)

    def code_filter(part):
        def step(i, _):
            cols = pl.ds(pl.multiple_of(i * 128, 128), 128)
            for j in range(2):
                tile = FILTER_CODE.encode(filt_ref[2 * part + j, :, cols].T)
                h_send[part, pl.ds(i * per_tile, per_tile), j] = tile.reshape(per_tile, own, rows)
            return 0

        lax.fori_loop(0, tiles, step, 0)

    def exchange(src, dst, sems):
        def step(i, _):
            to = lax.rem(me + i, n)
            pltpu.make_async_remote_copy(
                src_ref=src.at[to], dst_ref=dst.at[me], send_sem=sems.at[0], recv_sem=sems.at[1],
                device_id=(to, column), device_id_type=MESH,
            ).start()
            return 0

        lax.fori_loop(1, n, step, 0)
        dst[pl.ds(me, 1)] = src[pl.ds(me, 1)]

    def landed(src, dst, sems):
        return pltpu.make_async_remote_copy(
            src_ref=src.at[pl.ds(0, n - 1)], dst_ref=dst.at[pl.ds(0, n - 1)], send_sem=sems.at[0], recv_sem=sems.at[1],
            device_id=(ahead, column), device_id_type=MESH,
        )

    code_filter(0)
    pl.semaphore_wait(barrier, n - 1 + n_ch - 1)
    halo = pltpu.make_async_remote_copy(
        src_ref=halo_send, dst_ref=halo_recv, send_sem=halo_sems.at[0], recv_sem=halo_sems.at[1],
        device_id=(ahead, column), device_id_type=MESH,
    )
    halo.start()
    exchange(h_send.at[0], h_recv.at[0], h_sems.at[0])
    code_filter(1)
    halo.wait()
    inside = jnp.where(me > 0, 1.0, 0.0)
    for i in range(3):
        ext[i, 6:8, :] = halo_recv[2 * i : 2 * i + 2, :] * inside

    def bounds(cols):
        size = [
            sum(jnp.abs(taps_ref[3 * i + lag : 3 * i + lag + 1, cols]) for lag in range(3)) * IN_MAX for i in (1, 2)
        ]
        return jnp.maximum(size[0] * size[1], 1e-30)

    def mix(i, _):
        cols = pl.ds(pl.multiple_of(i * 128, 128), 128)

        def short(which):
            return sum(
                taps_ref[3 * which + lag : 3 * which + lag + 1, cols] * ext[which, 8 - lag : 8 - lag + rows, cols]
                for lag in range(3)
            )

        query[:, cols] = short(0)
        value = short(1) * short(2)
        mixed[:, cols] = value
        code = MIXED_CODE.encode((value / bounds(cols)).T)
        x_send[pl.ds(i * per_tile, per_tile)] = code.reshape(per_tile, own, rows)
        return 0

    lax.fori_loop(0, tiles, mix, 0)
    exchange(x_send, x_recv, x_sems)
    exchange(h_send.at[1], h_recv.at[1], h_sems.at[1])
    landed(x_send, x_recv, x_sems).wait()

    half = 2 * n

    def widen(i, _):
        at = pl.ds(pl.multiple_of(i * own, own), own)
        work[at, :] = MIXED_CODE.decode(x_recv[i])
        return 0

    lax.fori_loop(0, n, widen, 0)

    def over_blocks(c, _):
        x = split(work[pl.ds(c, n, stride=own), :])
        y = dot3((outer_ref[0], outer_ref[1]), x)
        re, im = y[:half], y[half:]
        cos, sin = tw_ref[0], tw_ref[1]
        spec_re[pl.ds(c, half, stride=own), :] = re * cos + im * sin
        spec_im[pl.ds(c, half, stride=own), :] = im * cos - re * sin
        return 0

    lax.fori_loop(0, own, over_blocks, 0)

    def over_rows(at, mat):
        re = split(spec_re[at, :])
        im = split(spec_im[at, :])
        both = tuple(jnp.concatenate((a, b), axis=1) for a, b in zip(re, im))
        return dot3(both, (mat[0], mat[1]))

    step_rows = min(256, half * own)
    steps = half * own // step_rows

    def forward(i, _):
        at = pl.ds(pl.multiple_of(i * step_rows, step_rows), step_rows)
        x = over_rows(at, fwd_ref)
        spec_re[at, :] = x[:, :rows]
        spec_im[at, :] = x[:, rows:]
        return 0

    lax.fori_loop(0, steps, forward, 0)

    for part in range(2):
        landed(h_send.at[part], h_recv.at[part], h_sems.at[part]).wait()

    def multiply(i, _):
        size = 2 * own
        at = pl.ds(pl.multiple_of(i * size, size), size)
        f_re = FILTER_CODE.decode(h_recv[0, i].reshape(size, rows))
        f_im = FILTER_CODE.decode(h_recv[1, i].reshape(size, rows))
        re, im = spec_re[at, :], spec_im[at, :]
        spec_re[at, :] = re * f_re - im * f_im
        spec_im[at, :] = re * f_im + im * f_re
        return 0

    lax.fori_loop(0, n, multiply, 0)

    def backward(i, _):
        at = pl.ds(pl.multiple_of(i * step_rows, step_rows), step_rows)
        x = over_rows(at, inv_ref)
        spec_re[at, :] = x[:, :rows]
        spec_im[at, :] = x[:, rows:]
        return 0

    lax.fori_loop(0, steps, backward, 0)

    def back_over_blocks(c, _):
        re, im = spec_re[pl.ds(c, half, stride=own), :], spec_im[pl.ds(c, half, stride=own), :]
        cos, sin = tw_ref[0], tw_ref[1]
        turned = jnp.concatenate((re * cos - im * sin, im * cos + re * sin), axis=0)
        work[pl.ds(c, n, stride=own), :] = dot3((inner_ref[0], inner_ref[1]), split(turned))
        return 0

    lax.fori_loop(0, own, back_over_blocks, 0)

    def narrow(i, _):
        at = pl.ds(pl.multiple_of(i * own, own), own)
        y_send[i] = CONV_CODE.encode(work[at, :])
        return 0

    lax.fori_loop(0, n, narrow, 0)
    exchange(y_send, y_recv, y_sems)
    landed(y_send, y_recv, y_sems).wait()

    sums[...] = jnp.zeros_like(sums)

    def gate(i, total):
        cols = pl.ds(pl.multiple_of(i * 128, 128), 128)
        conv = CONV_CODE.decode(y_recv[pl.ds(i * per_tile, per_tile)].reshape(128, rows)).T * bounds(cols)
        gated = query[:, cols] * (conv + skip_ref[:, cols] * mixed[:, cols])
        query[:, cols] = gated
        return total + gated * gated

    total = lax.fori_loop(0, tiles, gate, jnp.zeros((rows, 128), F32))
    sums[0:1, :] = jnp.sum(total.T, axis=0, keepdims=True)
    sends = []
    for i in range(1, n_ch):
        copy = pltpu.make_async_remote_copy(
            src_ref=sums, dst_ref=sums_recv.at[i], send_sem=sum_send.at[i], recv_sem=sum_recv.at[i],
            device_id=(me, lax.rem(column + i, n_ch)), device_id_type=MESH,
        )
        copy.start()
        sends.append(copy)
    square = sums[0:1, :]
    for i, copy in enumerate(sends):
        copy.wait()
        square = square + sums_recv[i + 1, 0:1, :]
    scale = lax.rsqrt(square / channels + EPS)
    scale = jnp.broadcast_to(scale, (128, rows)).T

    def finish(i, _):
        cols = pl.ds(pl.multiple_of(i * 128, 128), 128)
        out_ref[:, cols] = (query[:, cols] * scale * gain_ref[:, cols]).astype(BF16)
        return 0

    lax.fori_loop(0, tiles, finish, 0)


def per_device(q_in, k_in, v_in, short_taps, skip_bias, norm_gain, filter_spectrum):
    rows, width = q_in.shape
    n, n_ch = lax.axis_size("ctx"), lax.axis_size("ch")
    own = width // n
    half = 2 * n
    consts = tables(n, rows)
    vmem = pl.BlockSpec(memory_space=pltpu.VMEM)
    dma = pltpu.SemaphoreType.DMA
    return pl.pallas_call(
        functools.partial(kernel, n, n_ch, float(width * n_ch)),
        out_shape=jax.ShapeDtypeStruct((rows, width), BF16),
        in_specs=[vmem] * (7 + len(consts)),
        out_specs=vmem,
        scratch_shapes=[
            pltpu.VMEM((3, rows + 8, width), F32),
            pltpu.VMEM((8, width), F32),
            pltpu.VMEM((8, width), F32),
            pltpu.VMEM((rows, width), F32),
            pltpu.VMEM((rows, width), F32),
            pltpu.VMEM((n, own, rows), BF16),
            pltpu.VMEM((n, own, rows), BF16),
            pltpu.VMEM((2, n, 2, own, rows), BF16),
            pltpu.VMEM((2, n, 2, own, rows), BF16),
            pltpu.VMEM((n, own, rows), BF16),
            pltpu.VMEM((n, own, rows), BF16),
            pltpu.VMEM((n * own, rows), F32),
            pltpu.VMEM((half * own, rows), F32),
            pltpu.VMEM((half * own, rows), F32),
            pltpu.VMEM((8, 128), F32),
            pltpu.VMEM((n_ch, 8, 128), F32),
            dma((2,)),
            dma((2,)),
            dma((2, 2)),
            dma((2,)),
            dma((n_ch,)),
            dma((n_ch,)),
        ],
        compiler_params=pltpu.CompilerParams(
            collective_id=0, has_side_effects=True, vmem_limit_bytes=56 * 2**20
        ),
    )(
        q_in, k_in, v_in,
        short_taps.reshape(-1, width), skip_bias[None], norm_gain[None],
        filter_spectrum.reshape(4, rows, width),
        *(jnp.asarray(c) for c in consts),
    )


def solution(mesh):
    placed = (
        P("ctx", "ch"),
        P("ctx", "ch"),
        P("ctx", "ch"),
        P(None, None, "ch"),
        P("ch"),
        P("ch"),
        P(None, "ctx", None, None, "ch"),
    )
    return jax.shard_map(
        per_device, mesh=mesh, in_specs=placed, out_specs=P("ctx", "ch"), check_vma=False
    )
```

```python
import functools

import jax
import jax.numpy as jnp
import numpy as np
from jax import lax
from jax.experimental import pallas as pl
from jax.experimental.pallas import tpu as pltpu
from jax.sharding import PartitionSpec as P

MESH = pl.DeviceIdType.MESH
F32 = jnp.float32
BF16 = jnp.bfloat16
EPS = 1e-06
BIAS = 120.0
LN2 = float(np.log(2.0))
IN_MAX = 6.0
GROUPS = 4


class Code:
    def __init__(self, power, top):
        self.power = power
        self.a = (2.0 ** (2.0 * BIAS / power) - 1.0) / top
        self.top = top

    def encode(self, x):
        size = jnp.minimum(jnp.abs(x), self.top)
        size = jnp.exp2((self.power / LN2) * jnp.log(1.0 + self.a * size) - BIAS)
        return jnp.where(x < 0.0, -size, size).astype(BF16)

    def decode(self, code):
        v = code.astype(F32)
        size = jnp.exp2((1.0 / (LN2 * self.power)) * jnp.log(jnp.abs(v)) + BIAS / self.power)
        size = (size - 1.0) * (1.0 / self.a)
        return jnp.where(v < 0.0, -size, size)


FILTER_CODE = Code(30.0, 6.0)
MIXED_CODE = Code(22.0, 1.0)
CONV_CODE = Code(14.0, 768.0)


def split(x):
    high = x.astype(BF16)
    return high, (x - high.astype(F32)).astype(BF16)


def dot(a, b):
    return jnp.dot(a, b, preferred_element_type=F32)


def tables(devices, rows):
    levels = devices.bit_length() - 1
    rev = np.array([int(format(e, f"0{levels}b")[::-1], 2) if levels else 0 for e in range(devices)])
    freq = (2 * rev[:, None] + np.arange(2)[None, :]).reshape(-1)
    blocks = 2 * devices
    full = blocks * rows
    turn = 2.0 * np.pi
    ang = turn * ((freq[:, None] * np.arange(devices)[None, :]) % blocks) / blocks
    outer = np.concatenate((np.cos(ang), -np.sin(ang)), 0)
    tw = turn * ((freq[:, None] * np.arange(rows)[None, :]) % full) / full
    ids = np.arange(rows)
    loc = turn * ((ids[:, None] * ids[None, :]) % rows) / rows
    c, s = np.cos(loc), np.sin(loc)

    def parts(m):
        m = m.astype(np.float32)
        high = m.astype(jnp.bfloat16)
        return high, (m - high.astype(np.float32)).astype(jnp.bfloat16)

    outer_high, outer_low = parts(outer)
    return (
        np.concatenate((outer_high, outer_high, outer_low), 1),
        np.concatenate(parts(outer.T / full), 0),
        np.stack(parts(np.block([[c, -s], [s, c]]))),
        np.stack(parts(np.block([[c, s], [-s, c]]))),
        np.stack((np.cos(tw), np.sin(tw))).astype(np.float32),
    )


def kernel(
    n, n_ch, channels,
    q_hbm, k_hbm, v_hbm, taps_hbm, skip_hbm, gain_hbm, filt_hbm, *rest,
):
    consts_hbm, rest = rest[:5], rest[5:]
    (
        out_ref,
        feats, taps_ref, skip_ref, gain_ref, filt, outer_ref, inner_ref, fwd_ref, inv_ref, tw_ref,
        ext, halo_send, halo_recv, query, mixed, x_send, x_recv, h_send, h_recv, y_send, y_recv,
        work, spec_re, spec_im, stage_high, stage_low, sums, sums_recv,
        in_sems, halo_sems, x_sems, h_send_sems, h_recv_sems, y_sems, sum_send, sum_recv,
    ) = rest
    me, column = lax.axis_index("ctx"), lax.axis_index("ch")
    rows, width = q_hbm.shape
    own = width // n
    part = own // 2
    half_width = width // 2
    tiles = half_width // 128
    per_tile = 128 // part
    blocks = 2 * n
    group = n // GROUPS
    ahead = lax.rem(me + 1, n)

    barrier = pltpu.get_barrier_semaphore()

    def greet(i, _):
        pl.semaphore_signal(barrier, inc=1, device_id=(lax.rem(me + i, n), column), device_id_type=MESH)
        return 0

    for i in range(1, n_ch):
        pl.semaphore_signal(barrier, inc=1, device_id=(me, lax.rem(column + i, n_ch)), device_id_type=MESH)
    lax.fori_loop(1, n, greet, 0)

    moves = [
        (filt_hbm.at[:, :, pl.ds(0, half_width)], filt.at[0]),
        (q_hbm, feats.at[0]),
        (k_hbm, feats.at[1]),
        (v_hbm, feats.at[2]),
        (taps_hbm, taps_ref),
        (filt_hbm.at[:, :, pl.ds(half_width, half_width)], filt.at[1]),
        *zip(consts_hbm, (outer_ref, inner_ref, fwd_ref, inv_ref, tw_ref)),
        (skip_hbm, skip_ref),
        (gain_hbm, gain_ref),
    ]
    loads = [pltpu.make_async_copy(src, dst, in_sems.at[i]) for i, (src, dst) in enumerate(moves)]
    for load in loads:
        load.start()

    def code_filter(h):
        def step(i, _):
            cols = pl.ds(pl.multiple_of(i * 128, 128), 128)
            for j in range(4):
                tile = FILTER_CODE.encode(filt[h, j, :, cols].T.reshape(per_tile, part, rows))
                h_send[h, pl.ds(i * per_tile, per_tile), j * part : (j + 1) * part] = tile
            return 0

        lax.fori_loop(0, tiles, step, 0)

    def send_filter(h):
        def step(i, _):
            to = lax.rem(me + i, n)
            pltpu.make_async_remote_copy(
                src_ref=h_send.at[h, to], dst_ref=h_recv.at[h, me],
                send_sem=h_send_sems.at[h], recv_sem=h_recv_sems.at[h, i // group],
                device_id=(to, column), device_id_type=MESH,
            ).start()
            return 0

        pltpu.make_async_copy(h_send.at[h, me], h_recv.at[h, me], h_recv_sems.at[h, 0]).start()
        lax.fori_loop(1, n, step, 0)

    def exchange(src, dst, sems):
        def step(i, _):
            to = lax.rem(me + i, n)
            pltpu.make_async_remote_copy(
                src_ref=src.at[to], dst_ref=dst.at[me], send_sem=sems.at[0], recv_sem=sems.at[1],
                device_id=(to, column), device_id_type=MESH,
            ).start()
            return 0

        lax.fori_loop(1, n, step, 0)
        dst[pl.ds(me, 1)] = src[pl.ds(me, 1)]

    def of_all(src, dst, send_sem, recv_sem, count):
        return pltpu.make_async_remote_copy(
            src_ref=src.at[pl.ds(0, count)], dst_ref=dst.at[pl.ds(0, count)], send_sem=send_sem, recv_sem=recv_sem,
            device_id=(ahead, column), device_id_type=MESH,
        )

    for load in loads[1:4]:
        load.wait()
    for i in range(3):
        ext[i, 8 : 8 + rows, :] = feats[i].astype(F32)
        halo_send[2 * i : 2 * i + 2, :] = ext[i, 6 + rows : 8 + rows, :]
    halo_send[6:8, :] = jnp.zeros((2, width), F32)
    sums[...] = jnp.zeros_like(sums)
    loads[0].wait()
    code_filter(0)
    pl.semaphore_wait(barrier, n - 1 + n_ch - 1)
    halo = pltpu.make_async_remote_copy(
        src_ref=halo_send, dst_ref=halo_recv, send_sem=halo_sems.at[0], recv_sem=halo_sems.at[1],
        device_id=(ahead, column), device_id_type=MESH,
    )
    halo.start()
    send_filter(0)
    loads[5].wait()
    code_filter(1)
    loads[4].wait()
    halo.wait()
    inside = jnp.where(me > 0, 1.0, 0.0)
    for i in range(3):
        ext[i, 6:8, :] = halo_recv[2 * i : 2 * i + 2, :] * inside

    def bounds(cols):
        size = [sum(jnp.abs(taps_ref[i, lag : lag + 1, cols]) for lag in range(3)) * IN_MAX for i in (1, 2)]
        return jnp.maximum(size[0] * size[1], 1e-30)

    for h in range(2):

        def mix(i, _, h=h):
            cols = pl.ds(pl.multiple_of(h * half_width + i * 128, 128), 128)

            def short(which):
                return sum(
                    taps_ref[which, lag : lag + 1, cols] * ext[which, 8 - lag : 8 - lag + rows, cols]
                    for lag in range(3)
                )

            query[:, cols] = short(0)
            value = short(1) * short(2)
            mixed[:, cols] = value
            code = MIXED_CODE.encode((value / bounds(cols)).T.reshape(per_tile, part, rows))
            x_send[pl.ds(i * per_tile, per_tile), h * part : (h + 1) * part] = code
            return 0

        lax.fori_loop(0, tiles, mix, 0)
    exchange(x_send, x_recv, x_sems)
    send_filter(1)
    for load in loads[6:]:
        load.wait()
    of_all(x_send, x_recv, x_sems.at[0], x_sems.at[1], n - 1).wait()

    def widen(i, _):
        at = pl.ds(pl.multiple_of(i * own, own), own)
        work[at, :] = MIXED_CODE.decode(x_recv[i])
        return 0

    lax.fori_loop(0, n, widen, 0)
    half_rows = blocks * part

    for h in range(2):

        def over_blocks(c, _, h=h):
            x = jnp.concatenate(
                [work[pl.ds(h * part + 2 * c + u, n, stride=own), :] for u in range(2)], axis=1
            )
            high, low = split(x)
            y = dot(outer_ref[...], jnp.concatenate((high, low, high), axis=0))
            cos, sin = tw_ref[0], tw_ref[1]
            for u in range(2):
                re, im = y[:blocks, u * rows : (u + 1) * rows], y[blocks:, u * rows : (u + 1) * rows]
                at = pl.ds(h * half_rows + 2 * c + u, blocks, stride=part)
                spec_re[at, :] = re * cos + im * sin
                spec_im[at, :] = im * cos - re * sin
            return 0

        lax.fori_loop(0, part // 2, over_blocks, 0)

    def over_rows(high, low, mat):
        return dot(high, mat[0]) + (dot(high, mat[1]) + dot(low, mat[0]))

    step_rows = min(256, half_rows)

    def forward(i, _):
        at = pl.ds(pl.multiple_of(i * step_rows, step_rows), step_rows)
        high, low = split(jnp.concatenate((spec_re[at, :], spec_im[at, :]), axis=1))
        x = over_rows(high, low, fwd_ref)
        spec_re[at, :] = x[:, :rows]
        spec_im[at, :] = x[:, rows:]
        return 0

    lax.fori_loop(0, 2 * half_rows // step_rows, forward, 0)

    size = 2 * part
    for h in range(2):

        def backward(g, _, h=h):
            of_all(
                h_send.at[h], h_recv.at[h], h_send_sems.at[h], h_recv_sems.at[h, g], group
            ).wait_recv()

            def place(u):
                e = lax.rem(me - (g * group + u) + n, n)
                return e, pl.ds(pl.multiple_of(h * half_rows + e * size, size), size)

            for u in range(group):
                e, at = place(u)
                f_re = FILTER_CODE.decode(h_recv[h, e, :size])
                f_im = FILTER_CODE.decode(h_recv[h, e, size:])
                re, im = spec_re[at, :], spec_im[at, :]
                high, low = split(jnp.concatenate((re * f_re - im * f_im, re * f_im + im * f_re), axis=1))
                stage_high[u * size : (u + 1) * size, :] = high
                stage_low[u * size : (u + 1) * size, :] = low
            x = over_rows(stage_high[...], stage_low[...], inv_ref)
            for u in range(group):
                _, at = place(u)
                spec_re[at, :] = x[u * size : (u + 1) * size, :rows]
                spec_im[at, :] = x[u * size : (u + 1) * size, rows:]
            return 0

        lax.fori_loop(0, GROUPS, backward, 0)

        def back_over_blocks(c, _, h=h):
            cos, sin = tw_ref[0], tw_ref[1]
            turned = []
            for u in range(2):
                at = pl.ds(h * half_rows + 2 * c + u, blocks, stride=part)
                re, im = spec_re[at, :], spec_im[at, :]
                turned.append(jnp.concatenate((re * cos - im * sin, im * cos + re * sin), axis=0))
            high, low = split(jnp.concatenate(turned, axis=1))
            y = dot(inner_ref[...], high)
            y = y[:n] + (y[n:] + dot(inner_ref[:n, :], low))
            for u in range(2):
                work[pl.ds(2 * c + u, n, stride=part), :] = y[:, u * rows : (u + 1) * rows]
            return 0

        lax.fori_loop(0, part // 2, back_over_blocks, 0)

        def narrow(i, _, h=h):
            at = pl.ds(pl.multiple_of(i * 8 * part, 8 * part), 8 * part)
            y_send[h, pl.ds(i * 8, 8)] = CONV_CODE.encode(work[at, :].reshape(8, part, rows))
            return 0

        lax.fori_loop(0, n // 8, narrow, 0)
        exchange(y_send.at[h], y_recv.at[h], y_sems.at[h])

    total = jnp.zeros((rows, 128), F32)
    for h in range(2):
        of_all(y_send.at[h], y_recv.at[h], y_sems.at[h, 0], y_sems.at[h, 1], n - 1).wait()

        def gate(i, total, h=h):
            cols = pl.ds(pl.multiple_of(h * half_width + i * 128, 128), 128)
            conv = CONV_CODE.decode(y_recv[h, pl.ds(i * per_tile, per_tile)]).reshape(128, rows).T * bounds(cols)
            gated = query[:, cols] * (conv + skip_ref[:, cols] * mixed[:, cols])
            query[:, cols] = gated
            return total + gated * gated

        total = lax.fori_loop(0, tiles, gate, total)
    sums[0:1, :] = jnp.sum(total.T, axis=0, keepdims=True)
    sends = []
    for i in range(1, n_ch):
        copy = pltpu.make_async_remote_copy(
            src_ref=sums, dst_ref=sums_recv.at[i], send_sem=sum_send.at[i], recv_sem=sum_recv.at[i],
            device_id=(me, lax.rem(column + i, n_ch)), device_id_type=MESH,
        )
        copy.start()
        sends.append(copy)
    for h in range(2):
        of_all(h_send.at[h], h_recv.at[h], h_send_sems.at[h], h_recv_sems.at[h, 0], n - 1).wait_send()
    square = sums[0:1, :]
    for i, copy in enumerate(sends):
        copy.wait()
        square = square + sums_recv[i + 1, 0:1, :]
    scale = lax.rsqrt(square / channels + EPS)
    scale = jnp.broadcast_to(scale, (128, rows)).T

    def finish(i, _):
        cols = pl.ds(pl.multiple_of(i * 128, 128), 128)
        out_ref[:, cols] = (query[:, cols] * scale * gain_ref[:, cols]).astype(BF16)
        return 0

    lax.fori_loop(0, 2 * tiles, finish, 0)


def per_device(q_in, k_in, v_in, short_taps, skip_bias, norm_gain, filter_spectrum):
    rows, width = q_in.shape
    n, n_ch = lax.axis_size("ctx"), lax.axis_size("ch")
    own = width // n
    part = own // 2
    blocks = 2 * n
    consts = tables(n, rows)
    anywhere = pl.BlockSpec(memory_space=pl.ANY)
    dma = pltpu.SemaphoreType.DMA
    like = [pltpu.VMEM(c.shape, c.dtype) for c in consts]
    return pl.pallas_call(
        functools.partial(kernel, n, n_ch, float(width * n_ch)),
        out_shape=jax.ShapeDtypeStruct((rows, width), BF16),
        in_specs=[anywhere] * (7 + len(consts)),
        out_specs=pl.BlockSpec(memory_space=pltpu.VMEM),
        scratch_shapes=[
            pltpu.VMEM((3, rows, width), BF16),
            pltpu.VMEM(short_taps.shape, F32),
            pltpu.VMEM((1, width), F32),
            pltpu.VMEM((1, width), F32),
            pltpu.VMEM((2, 4, rows, width // 2), F32),
            *like,
            pltpu.VMEM((3, rows + 8, width), F32),
            pltpu.VMEM((8, width), F32),
            pltpu.VMEM((8, width), F32),
            pltpu.VMEM((rows, width), F32),
            pltpu.VMEM((rows, width), F32),
            pltpu.VMEM((n, own, rows), BF16),
            pltpu.VMEM((n, own, rows), BF16),
            pltpu.VMEM((2, n, 4 * part, rows), BF16),
            pltpu.VMEM((2, n, 4 * part, rows), BF16),
            pltpu.VMEM((2, n, part, rows), BF16),
            pltpu.VMEM((2, n, part, rows), BF16),
            pltpu.VMEM((n * own, rows), F32),
            pltpu.VMEM((blocks * own, rows), F32),
            pltpu.VMEM((blocks * own, rows), F32),
            pltpu.VMEM((n // GROUPS * own, 2 * rows), BF16),
            pltpu.VMEM((n // GROUPS * own, 2 * rows), BF16),
            pltpu.VMEM((8, 128), F32),
            pltpu.VMEM((n_ch, 8, 128), F32),
            dma((13,)),
            dma((2,)),
            dma((2,)),
            dma((2,)),
            dma((2, GROUPS)),
            dma((2, 2)),
            dma((n_ch,)),
            dma((n_ch,)),
        ],
        compiler_params=pltpu.CompilerParams(
            collective_id=0, has_side_effects=True, vmem_limit_bytes=56 * 2**20
        ),
    )(
        q_in, k_in, v_in, short_taps, skip_bias[None], norm_gain[None],
        filter_spectrum.reshape(4, rows, width),
        *(jnp.asarray(c) for c in consts),
    )


def solution(mesh):
    placed = (
        P("ctx", "ch"),
        P("ctx", "ch"),
        P("ctx", "ch"),
        P(None, None, "ch"),
        P("ch"),
        P("ch"),
        P(None, "ctx", None, None, "ch"),
    )
    return jax.shard_map(
        per_device, mesh=mesh, in_specs=placed, out_specs=P("ctx", "ch"), check_vma=False
    )
```

```python
import functools

import jax
import jax.numpy as jnp
import numpy as np
from jax import lax
from jax.experimental import pallas as pl
from jax.experimental.pallas import tpu as pltpu
from jax.sharding import PartitionSpec as P

MESH = pl.DeviceIdType.MESH
F32 = jnp.float32
BF16 = jnp.bfloat16
EPS = 1e-06
BIAS = 125.0
LN2 = float(np.log(2.0))
IN_MAX = 6.0
PARTS = 4
GROUPS = 4


class Code:
    def __init__(self, power, top):
        self.power = power
        self.a = (2.0 ** (2.0 * BIAS / power) - 1.0) / top
        self.top = top

    def encode(self, x):
        size = jnp.minimum(jnp.abs(x), self.top)
        size = jnp.exp2((self.power / LN2) * jnp.log(1.0 + self.a * size) - BIAS)
        return jnp.where(x < 0.0, -size, size).astype(BF16)

    def decode(self, code):
        v = code.astype(F32)
        size = jnp.exp2((1.0 / (LN2 * self.power)) * jnp.log(jnp.abs(v)) + BIAS / self.power)
        size = (size - 1.0) * (1.0 / self.a)
        return jnp.where(v < 0.0, -size, size)


FILTER_CODE = Code(30.0, 6.0)
MIXED_CODE = Code(15.0, 1.0)
CONV_CODE = Code(10.5, 768.0)


def split(x):
    high = x.astype(BF16)
    return high, (x - high.astype(F32)).astype(BF16)


def dot(a, b):
    return jnp.dot(a, b, preferred_element_type=F32)


def tables(devices, rows):
    levels = devices.bit_length() - 1
    rev = np.array([int(format(e, f"0{levels}b")[::-1], 2) if levels else 0 for e in range(devices)])
    freq = (2 * rev[:, None] + np.arange(2)[None, :]).reshape(-1)
    blocks = 2 * devices
    full = blocks * rows
    turn = 2.0 * np.pi
    ang = turn * ((freq[:, None] * np.arange(devices)[None, :]) % blocks) / blocks
    outer = np.concatenate((np.cos(ang), -np.sin(ang)), 0)
    tw = turn * ((freq[:, None] * np.arange(rows)[None, :]) % full) / full
    ids = np.arange(rows)
    loc = turn * ((ids[:, None] * ids[None, :]) % rows) / rows
    c, s = np.cos(loc), np.sin(loc)

    def parts(m):
        m = m.astype(np.float32)
        high = m.astype(jnp.bfloat16)
        return high, (m - high.astype(np.float32)).astype(jnp.bfloat16)

    outer_high, outer_low = parts(outer)
    return (
        np.concatenate((outer_high, outer_high, outer_low), 1),
        np.concatenate(parts(outer.T / full), 0),
        np.stack(parts(np.block([[c, -s], [s, c]]))),
        np.stack(parts(np.block([[c, s], [-s, c]]))),
        np.stack((np.cos(tw), np.sin(tw))).astype(np.float32),
    )


def kernel(
    n, n_ch, channels,
    q_hbm, k_hbm, v_hbm, taps_hbm, skip_hbm, gain_hbm, filt_hbm, *rest,
):
    consts_hbm, rest = rest[:5], rest[5:]
    (
        out_ref,
        feats, taps_ref, skip_ref, gain_ref, filt, outer_ref, inner_ref, fwd_ref, inv_ref, tw_ref,
        ext, halo_send, halo_recv, query, mixed, x_send, x_recv, h_send, h_recv, y_send, y_recv,
        work, spec_re, spec_im, stage_high, stage_low, sums, sums_recv,
        in_sems, halo_sems, x_sems, h_send_sems, h_recv_sems, y_sems, sum_send, sum_recv,
    ) = rest
    me, column = lax.axis_index("ctx"), lax.axis_index("ch")
    rows, width = q_hbm.shape
    own = width // n
    part = own // PARTS
    part_width = width // PARTS
    tiles = part_width // 128
    per_tile = 128 // part
    blocks = 2 * n
    group = n // GROUPS
    ahead = lax.rem(me + 1, n)

    barrier = pltpu.get_barrier_semaphore()

    def greet(i, _):
        pl.semaphore_signal(barrier, inc=1, device_id=(lax.rem(me + i, n), column), device_id_type=MESH)
        return 0

    for i in range(1, n_ch):
        pl.semaphore_signal(barrier, inc=1, device_id=(me, lax.rem(column + i, n_ch)), device_id_type=MESH)
    lax.fori_loop(1, n, greet, 0)

    moves = [
        *((filt_hbm.at[:, :, pl.ds(h * part_width, part_width)], filt.at[h]) for h in range(PARTS)),
        (q_hbm, feats.at[0]),
        (k_hbm, feats.at[1]),
        (v_hbm, feats.at[2]),
        (taps_hbm, taps_ref),
        *zip(consts_hbm, (outer_ref, inner_ref, fwd_ref, inv_ref, tw_ref)),
        (skip_hbm, skip_ref),
        (gain_hbm, gain_ref),
    ]
    loads = [pltpu.make_async_copy(src, dst, in_sems.at[i]) for i, (src, dst) in enumerate(moves)]
    for load in loads:
        load.start()

    def code_filter(h):
        def step(i, _):
            cols = pl.ds(pl.multiple_of(i * 128, 128), 128)
            for j in range(4):
                tile = FILTER_CODE.encode(filt[h, j, :, cols].T.reshape(per_tile, part, rows))
                h_send[h, pl.ds(i * per_tile, per_tile), j * part : (j + 1) * part] = tile
            return 0

        lax.fori_loop(0, tiles, step, 0)

    def send_filter(h):
        def step(i, _):
            to = lax.rem(me + i, n)
            pltpu.make_async_remote_copy(
                src_ref=h_send.at[h, to], dst_ref=h_recv.at[h, me],
                send_sem=h_send_sems.at[h], recv_sem=h_recv_sems.at[h, i // group],
                device_id=(to, column), device_id_type=MESH,
            ).start()
            return 0

        pltpu.make_async_copy(h_send.at[h, me], h_recv.at[h, me], h_recv_sems.at[h, 0]).start()
        lax.fori_loop(1, n, step, 0)

    def exchange(src, dst, sems):
        def step(i, _):
            to = lax.rem(me + i, n)
            pltpu.make_async_remote_copy(
                src_ref=src.at[to], dst_ref=dst.at[me], send_sem=sems.at[0], recv_sem=sems.at[1],
                device_id=(to, column), device_id_type=MESH,
            ).start()
            return 0

        lax.fori_loop(1, n, step, 0)
        dst[pl.ds(me, 1)] = src[pl.ds(me, 1)]

    def of_all(src, dst, send_sem, recv_sem, count):
        return pltpu.make_async_remote_copy(
            src_ref=src.at[pl.ds(0, count)], dst_ref=dst.at[pl.ds(0, count)], send_sem=send_sem, recv_sem=recv_sem,
            device_id=(ahead, column), device_id_type=MESH,
        )

    for load in loads[PARTS : PARTS + 3]:
        load.wait()
    for i in range(3):
        ext[i, 8 : 8 + rows, :] = feats[i].astype(F32)
        halo_send[2 * i : 2 * i + 2, :] = ext[i, 6 + rows : 8 + rows, :]
    halo_send[6:8, :] = jnp.zeros((2, width), F32)
    sums[...] = jnp.zeros_like(sums)
    loads[0].wait()
    code_filter(0)
    pl.semaphore_wait(barrier, n - 1 + n_ch - 1)
    halo = pltpu.make_async_remote_copy(
        src_ref=halo_send, dst_ref=halo_recv, send_sem=halo_sems.at[0], recv_sem=halo_sems.at[1],
        device_id=(ahead, column), device_id_type=MESH,
    )
    halo.start()
    send_filter(0)
    for h in range(1, PARTS):
        loads[h].wait()
        code_filter(h)
    loads[PARTS + 3].wait()
    halo.wait()
    inside = jnp.where(me > 0, 1.0, 0.0)
    for i in range(3):
        ext[i, 6:8, :] = halo_recv[2 * i : 2 * i + 2, :] * inside

    def bounds(cols):
        size = [sum(jnp.abs(taps_ref[i, lag : lag + 1, cols]) for lag in range(3)) * IN_MAX for i in (1, 2)]
        return jnp.maximum(size[0] * size[1], 1e-30)

    for h in range(PARTS):

        def mix(i, _, h=h):
            cols = pl.ds(pl.multiple_of(h * part_width + i * 128, 128), 128)

            def short(which):
                return sum(
                    taps_ref[which, lag : lag + 1, cols] * ext[which, 8 - lag : 8 - lag + rows, cols]
                    for lag in range(3)
                )

            query[:, cols] = short(0)
            value = short(1) * short(2)
            mixed[:, cols] = value
            code = MIXED_CODE.encode((value / bounds(cols)).T.reshape(per_tile, part, rows))
            x_send[pl.ds(i * per_tile, per_tile), h * part : (h + 1) * part] = code
            return 0

        lax.fori_loop(0, tiles, mix, 0)
    exchange(x_send, x_recv, x_sems)
    send_filter(1)
    for load in loads[PARTS + 4 :]:
        load.wait()
    of_all(x_send, x_recv, x_sems.at[0], x_sems.at[1], n - 1).wait()
    for h in range(2, PARTS):
        send_filter(h)

    def widen(i, _):
        at = pl.ds(pl.multiple_of(i * own, own), own)
        work[at, :] = MIXED_CODE.decode(x_recv[i])
        return 0

    lax.fori_loop(0, n, widen, 0)
    part_rows = blocks * part

    for h in range(PARTS):

        def over_blocks(c, _, h=h):
            x = jnp.concatenate(
                [work[pl.ds(h * part + 2 * c + u, n, stride=own), :] for u in range(2)], axis=1
            )
            high, low = split(x)
            y = dot(outer_ref[...], jnp.concatenate((high, low, high), axis=0))
            cos, sin = tw_ref[0], tw_ref[1]
            for u in range(2):
                re, im = y[:blocks, u * rows : (u + 1) * rows], y[blocks:, u * rows : (u + 1) * rows]
                at = pl.ds(h * part_rows + 2 * c + u, blocks, stride=part)
                spec_re[at, :] = re * cos + im * sin
                spec_im[at, :] = im * cos - re * sin
            return 0

        lax.fori_loop(0, part // 2, over_blocks, 0)

    def over_rows(high, low, mat):
        return dot(high, mat[0]) + (dot(high, mat[1]) + dot(low, mat[0]))

    step_rows = min(256, part_rows)

    def forward(i, _):
        at = pl.ds(pl.multiple_of(i * step_rows, step_rows), step_rows)
        high, low = split(jnp.concatenate((spec_re[at, :], spec_im[at, :]), axis=1))
        x = over_rows(high, low, fwd_ref)
        spec_re[at, :] = x[:, :rows]
        spec_im[at, :] = x[:, rows:]
        return 0

    lax.fori_loop(0, PARTS * part_rows // step_rows, forward, 0)

    size = 2 * part
    for h in range(PARTS):

        def backward(g, _, h=h):
            of_all(
                h_send.at[h], h_recv.at[h], h_send_sems.at[h], h_recv_sems.at[h, g], group
            ).wait_recv()

            def place(u):
                e = lax.rem(me - (g * group + u) + n, n)
                return e, pl.ds(pl.multiple_of(h * part_rows + e * size, size), size)

            for u in range(group):
                e, at = place(u)
                f_re = FILTER_CODE.decode(h_recv[h, e, :size])
                f_im = FILTER_CODE.decode(h_recv[h, e, size:])
                re, im = spec_re[at, :], spec_im[at, :]
                high, low = split(jnp.concatenate((re * f_re - im * f_im, re * f_im + im * f_re), axis=1))
                stage_high[u * size : (u + 1) * size, :] = high
                stage_low[u * size : (u + 1) * size, :] = low
            x = over_rows(stage_high[...], stage_low[...], inv_ref)
            for u in range(group):
                _, at = place(u)
                spec_re[at, :] = x[u * size : (u + 1) * size, :rows]
                spec_im[at, :] = x[u * size : (u + 1) * size, rows:]
            return 0

        lax.fori_loop(0, GROUPS, backward, 0)

        def back_over_blocks(c, _, h=h):
            cos, sin = tw_ref[0], tw_ref[1]
            turned = []
            for u in range(2):
                at = pl.ds(h * part_rows + 2 * c + u, blocks, stride=part)
                re, im = spec_re[at, :], spec_im[at, :]
                turned.append(jnp.concatenate((re * cos - im * sin, im * cos + re * sin), axis=0))
            high, low = split(jnp.concatenate(turned, axis=1))
            y = dot(inner_ref[...], high)
            y = y[:n] + (y[n:] + dot(inner_ref[:n, :], low))
            for u in range(2):
                work[pl.ds(2 * c + u, n, stride=part), :] = y[:, u * rows : (u + 1) * rows]
            return 0

        lax.fori_loop(0, part // 2, back_over_blocks, 0)

        def narrow(i, _, h=h):
            at = pl.ds(pl.multiple_of(i * 8 * part, 8 * part), 8 * part)
            y_send[h, pl.ds(i * 8, 8)] = CONV_CODE.encode(work[at, :].reshape(8, part, rows))
            return 0

        lax.fori_loop(0, n // 8, narrow, 0)
        exchange(y_send.at[h], y_recv.at[h], y_sems.at[h])

    total = jnp.zeros((rows, 128), F32)
    for h in range(PARTS):
        of_all(y_send.at[h], y_recv.at[h], y_sems.at[h, 0], y_sems.at[h, 1], n - 1).wait()

        def gate(i, total, h=h):
            cols = pl.ds(pl.multiple_of(h * part_width + i * 128, 128), 128)
            conv = CONV_CODE.decode(y_recv[h, pl.ds(i * per_tile, per_tile)]).reshape(128, rows).T * bounds(cols)
            gated = query[:, cols] * (conv + skip_ref[:, cols] * mixed[:, cols])
            query[:, cols] = gated
            return total + gated * gated

        total = lax.fori_loop(0, tiles, gate, total)
    sums[0:1, :] = jnp.sum(total.T, axis=0, keepdims=True)
    sends = []
    for i in range(1, n_ch):
        copy = pltpu.make_async_remote_copy(
            src_ref=sums, dst_ref=sums_recv.at[i], send_sem=sum_send.at[i], recv_sem=sum_recv.at[i],
            device_id=(me, lax.rem(column + i, n_ch)), device_id_type=MESH,
        )
        copy.start()
        sends.append(copy)
    for h in range(PARTS):
        of_all(h_send.at[h], h_recv.at[h], h_send_sems.at[h], h_recv_sems.at[h, 0], n - 1).wait_send()
    square = sums[0:1, :]
    for i, copy in enumerate(sends):
        copy.wait()
        square = square + sums_recv[i + 1, 0:1, :]
    scale = lax.rsqrt(square / channels + EPS)
    scale = jnp.broadcast_to(scale, (128, rows)).T

    def finish(i, _):
        cols = pl.ds(pl.multiple_of(i * 128, 128), 128)
        out_ref[:, cols] = (query[:, cols] * scale * gain_ref[:, cols]).astype(BF16)
        return 0

    lax.fori_loop(0, PARTS * tiles, finish, 0)


def per_device(q_in, k_in, v_in, short_taps, skip_bias, norm_gain, filter_spectrum):
    rows, width = q_in.shape
    n, n_ch = lax.axis_size("ctx"), lax.axis_size("ch")
    own = width // n
    part = own // PARTS
    blocks = 2 * n
    consts = tables(n, rows)
    anywhere = pl.BlockSpec(memory_space=pl.ANY)
    dma = pltpu.SemaphoreType.DMA
    like = [pltpu.VMEM(c.shape, c.dtype) for c in consts]
    return pl.pallas_call(
        functools.partial(kernel, n, n_ch, float(width * n_ch)),
        out_shape=jax.ShapeDtypeStruct((rows, width), BF16),
        in_specs=[anywhere] * (7 + len(consts)),
        out_specs=pl.BlockSpec(memory_space=pltpu.VMEM),
        scratch_shapes=[
            pltpu.VMEM((3, rows, width), BF16),
            pltpu.VMEM(short_taps.shape, F32),
            pltpu.VMEM((1, width), F32),
            pltpu.VMEM((1, width), F32),
            pltpu.VMEM((PARTS, 4, rows, width // PARTS), F32),
            *like,
            pltpu.VMEM((3, rows + 8, width), F32),
            pltpu.VMEM((8, width), F32),
            pltpu.VMEM((8, width), F32),
            pltpu.VMEM((rows, width), F32),
            pltpu.VMEM((rows, width), F32),
            pltpu.VMEM((n, own, rows), BF16),
            pltpu.VMEM((n, own, rows), BF16),
            pltpu.VMEM((PARTS, n, 4 * part, rows), BF16),
            pltpu.VMEM((PARTS, n, 4 * part, rows), BF16),
            pltpu.VMEM((PARTS, n, part, rows), BF16),
            pltpu.VMEM((PARTS, n, part, rows), BF16),
            pltpu.VMEM((n * own, rows), F32),
            pltpu.VMEM((blocks * own, rows), F32),
            pltpu.VMEM((blocks * own, rows), F32),
            pltpu.VMEM((n // GROUPS * 2 * part, 2 * rows), BF16),
            pltpu.VMEM((n // GROUPS * 2 * part, 2 * rows), BF16),
            pltpu.VMEM((8, 128), F32),
            pltpu.VMEM((n_ch, 8, 128), F32),
            dma((11 + PARTS,)),
            dma((2,)),
            dma((2,)),
            dma((PARTS,)),
            dma((PARTS, GROUPS)),
            dma((PARTS, 2)),
            dma((n_ch,)),
            dma((n_ch,)),
        ],
        compiler_params=pltpu.CompilerParams(
            collective_id=0, has_side_effects=True, vmem_limit_bytes=56 * 2**20
        ),
    )(
        q_in, k_in, v_in, short_taps, skip_bias[None], norm_gain[None],
        filter_spectrum.reshape(4, rows, width),
        *(jnp.asarray(c) for c in consts),
    )


def solution(mesh):
    placed = (
        P("ctx", "ch"),
        P("ctx", "ch"),
        P("ctx", "ch"),
        P(None, None, "ch"),
        P("ch"),
        P("ch"),
        P(None, "ctx", None, None, "ch"),
    )
    return jax.shard_map(
        per_device, mesh=mesh, in_specs=placed, out_specs=P("ctx", "ch"), check_vma=False
    )
```

```python
import functools

import jax
import jax.numpy as jnp
import numpy as np
from jax import lax
from jax.experimental import pallas as pl
from jax.experimental.pallas import tpu as pltpu
from jax.sharding import PartitionSpec as P

MESH = pl.DeviceIdType.MESH
F32 = jnp.float32
BF16 = jnp.bfloat16
EPS = 1e-06
BIAS = 125.0
LN2 = float(np.log(2.0))
IN_MAX = 6.0
PARTS = 4
GROUPS = 4


class Code:
    def __init__(self, power, top, knee=None, tail=1.0):
        self.power, self.top, self.tail = power, top, tail
        self.knee = top if knee is None else knee
        self.turn = 2.0 * BIAS - tail * float(np.log2(top / self.knee))
        self.a = (2.0 ** (self.turn / power) - 1.0) / self.knee

    def encode(self, x):
        size = jnp.minimum(jnp.abs(x), self.top)
        inner = jnp.minimum(size, self.knee)
        code = (self.power / LN2) * jnp.log(1.0 + self.a * inner) - BIAS
        if self.knee < self.top:
            code = code + (self.tail / LN2) * jnp.log(jnp.maximum(size * (1.0 / self.knee), 1.0))
        code = jnp.exp2(code)
        return jnp.where(x < 0.0, -code, code).astype(BF16)

    def decode(self, code):
        v = code.astype(F32)
        size = (1.0 / LN2) * jnp.log(jnp.abs(v)) + BIAS
        inner = jnp.minimum(size, self.turn) if self.knee < self.top else size
        x = (jnp.exp2((1.0 / self.power) * inner) - 1.0) * (1.0 / self.a)
        if self.knee < self.top:
            x = x * jnp.exp2((1.0 / self.tail) * (size - inner))
        return jnp.where(v < 0.0, -x, x)


FILTER_CODE = Code(30.0, 6.0)
MIXED_CODE = Code(24.0, 1.0)
CONV_CODE = Code(15.4, 768.0, 4.0, 4.0)


def split(x):
    high = x.astype(BF16)
    return high, (x - high.astype(F32)).astype(BF16)


def dot(a, b):
    return jnp.dot(a, b, preferred_element_type=F32)


def tables(devices, rows):
    levels = devices.bit_length() - 1
    rev = np.array([int(format(e, f"0{levels}b")[::-1], 2) if levels else 0 for e in range(devices)])
    freq = (2 * rev[:, None] + np.arange(2)[None, :]).reshape(-1)
    blocks = 2 * devices
    full = blocks * rows
    turn = 2.0 * np.pi
    ang = turn * ((freq[:, None] * np.arange(devices)[None, :]) % blocks) / blocks
    outer = np.concatenate((np.cos(ang), -np.sin(ang)), 0)
    tw = turn * ((freq[:, None] * np.arange(rows)[None, :]) % full) / full
    ids = np.arange(rows)
    loc = turn * ((ids[:, None] * ids[None, :]) % rows) / rows
    c, s = np.cos(loc), np.sin(loc)

    def parts(m):
        m = m.astype(np.float32)
        high = m.astype(jnp.bfloat16)
        return high, (m - high.astype(np.float32)).astype(jnp.bfloat16)

    outer_high, outer_low = parts(outer)
    return (
        np.concatenate((outer_high, outer_high, outer_low), 1),
        np.concatenate(parts(outer.T / full), 0),
        np.stack(parts(np.block([[c, -s], [s, c]]))),
        np.stack(parts(np.block([[c, s], [-s, c]]))),
        np.stack((np.cos(tw), np.sin(tw))).astype(np.float32),
    )


def kernel(
    n, n_ch, channels,
    q_hbm, k_hbm, v_hbm, taps_hbm, skip_hbm, gain_hbm, filt_hbm, *rest,
):
    consts_hbm, rest = rest[:5], rest[5:]
    (
        out_ref,
        feats, taps_ref, skip_ref, gain_ref, filt, outer_ref, inner_ref, fwd_ref, inv_ref, tw_ref,
        ext, halo_send, halo_recv, query, mixed, x_send, x_recv, h_send, h_recv, y_send, y_recv,
        work, back, peaks, scale_send, scale_recv, spec_re, spec_im, stage_high, stage_low, sums, sums_recv,
        in_sems, halo_sems, scale_sems, x_sems, h_send_sems, h_recv_sems, y_sems, sum_send, sum_recv,
    ) = rest
    me, column = lax.axis_index("ctx"), lax.axis_index("ch")
    rows, width = q_hbm.shape
    own = width // n
    part = own // PARTS
    part_width = width // PARTS
    tiles = part_width // 128
    per_tile = 128 // part
    blocks = 2 * n
    group = n // GROUPS
    ahead = lax.rem(me + 1, n)

    barrier = pltpu.get_barrier_semaphore()

    def greet(i, _):
        pl.semaphore_signal(barrier, inc=1, device_id=(lax.rem(me + i, n), column), device_id_type=MESH)
        return 0

    for i in range(1, n_ch):
        pl.semaphore_signal(barrier, inc=1, device_id=(me, lax.rem(column + i, n_ch)), device_id_type=MESH)
    lax.fori_loop(1, n, greet, 0)

    moves = [
        *((filt_hbm.at[:, :, pl.ds(h * part_width, part_width)], filt.at[h]) for h in range(PARTS)),
        (q_hbm, feats.at[0]),
        (k_hbm, feats.at[1]),
        (v_hbm, feats.at[2]),
        (taps_hbm, taps_ref),
        *zip(consts_hbm, (outer_ref, inner_ref, fwd_ref, inv_ref, tw_ref)),
        (skip_hbm, skip_ref),
        (gain_hbm, gain_ref),
    ]
    loads = [pltpu.make_async_copy(src, dst, in_sems.at[i]) for i, (src, dst) in enumerate(moves)]
    for load in loads:
        load.start()

    def code_filter(h):
        def step(i, _):
            cols = pl.ds(pl.multiple_of(i * 128, 128), 128)
            tiles_of = [
                FILTER_CODE.encode(filt[h, j, :, cols].T.reshape(per_tile, part, rows)) for j in range(4)
            ]
            h_send[h, pl.ds(i * per_tile, per_tile)] = jnp.concatenate(tiles_of, axis=1)
            return 0

        lax.fori_loop(0, tiles, step, 0)

    def send_filter(h):
        def step(i, _):
            to = lax.rem(me + i, n)
            pltpu.make_async_remote_copy(
                src_ref=h_send.at[h, to], dst_ref=h_recv.at[h, me],
                send_sem=h_send_sems.at[h], recv_sem=h_recv_sems.at[h, i // group],
                device_id=(to, column), device_id_type=MESH,
            ).start()
            return 0

        pltpu.make_async_copy(h_send.at[h, me], h_recv.at[h, me], h_recv_sems.at[h, 0]).start()
        lax.fori_loop(1, n, step, 0)

    def exchange(src, dst, sems):
        def step(i, _):
            to = lax.rem(me + i, n)
            pltpu.make_async_remote_copy(
                src_ref=src.at[to], dst_ref=dst.at[me], send_sem=sems.at[0], recv_sem=sems.at[1],
                device_id=(to, column), device_id_type=MESH,
            ).start()
            return 0

        lax.fori_loop(1, n, step, 0)
        dst[pl.ds(me, 1)] = src[pl.ds(me, 1)]

    def of_all(src, dst, send_sem, recv_sem, count):
        return pltpu.make_async_remote_copy(
            src_ref=src.at[pl.ds(0, count)], dst_ref=dst.at[pl.ds(0, count)], send_sem=send_sem, recv_sem=recv_sem,
            device_id=(ahead, column), device_id_type=MESH,
        )

    for load in loads[PARTS : PARTS + 3]:
        load.wait()
    for i in range(3):
        ext[i, 8 : 8 + rows, :] = feats[i].astype(F32)
        halo_send[2 * i : 2 * i + 2, :] = ext[i, 6 + rows : 8 + rows, :]
    halo_send[6:8, :] = jnp.zeros((2, width), F32)
    for i in (1, 2):
        peaks[i : i + 1, :] = jnp.max(jnp.abs(ext[i, 8 : 8 + rows, :]), axis=0, keepdims=True)
    sums[...] = jnp.zeros_like(sums)
    loads[0].wait()
    code_filter(0)
    pl.semaphore_wait(barrier, n - 1 + n_ch - 1)
    halo = pltpu.make_async_remote_copy(
        src_ref=halo_send, dst_ref=halo_recv, send_sem=halo_sems.at[0], recv_sem=halo_sems.at[1],
        device_id=(ahead, column), device_id_type=MESH,
    )
    halo.start()
    send_filter(0)
    loads[1].wait()
    code_filter(1)
    loads[PARTS + 3].wait()
    halo.wait()
    inside = jnp.where(me > 0, 1.0, 0.0)
    for i in range(3):
        ext[i, 6:8, :] = halo_recv[2 * i : 2 * i + 2, :] * inside

    highest = [
        jnp.max(jnp.maximum(peaks[i : i + 1, :], jnp.max(jnp.abs(ext[i, 6:8, :]), axis=0, keepdims=True)), axis=1, keepdims=True)
        for i in (1, 2)
    ]
    bound = jnp.maximum(highest[0] * highest[1] * (1.0 / IN_MAX**2), 1e-30)
    scale_send[...] = jnp.broadcast_to(bound, (1, 128))

    def bounds(cols):
        size = [sum(jnp.abs(taps_ref[i, lag : lag + 1, cols]) for lag in range(3)) * IN_MAX for i in (1, 2)]
        return jnp.maximum(size[0] * size[1], 1e-30)

    def short(which, cols):
        return sum(
            taps_ref[which, lag : lag + 1, cols] * ext[which, 8 - lag : 8 - lag + rows, cols] for lag in range(3)
        )

    def columns(h, i):
        return pl.ds(pl.multiple_of(h * part_width + i * 128, 128), 128)

    def mix(i, _):
        codes = []
        for h in range(PARTS):
            cols = columns(h, i)
            value = short(1, cols) * short(2, cols)
            mixed[:, cols] = value
            value = (value / bounds(cols)) * (1.0 / scale_send[...])
            codes.append(MIXED_CODE.encode(value.T.reshape(per_tile, part, rows)))
        x_send[pl.ds(i * per_tile, per_tile)] = jnp.concatenate(codes, axis=1)
        return 0

    lax.fori_loop(0, tiles, mix, 0)

    def send_mixed(i, _):
        to = lax.rem(me + i, n)
        for src, dst, sems in ((scale_send, scale_recv, scale_sems), (x_send.at[to], x_recv, x_sems)):
            pltpu.make_async_remote_copy(
                src_ref=src, dst_ref=dst.at[me], send_sem=sems.at[0], recv_sem=sems.at[1],
                device_id=(to, column), device_id_type=MESH,
            ).start()
        return 0

    lax.fori_loop(1, n, send_mixed, 0)
    x_recv[pl.ds(me, 1)] = x_send[pl.ds(me, 1)]
    scale_recv[pl.ds(me, 1)] = scale_send[...].reshape(1, 1, 128)
    send_filter(1)
    for h in range(2, PARTS):
        loads[h].wait()
        code_filter(h)

    def gates(i, _):
        for h in range(PARTS):
            cols = columns(h, i)
            query[:, cols] = short(0, cols)
        return 0

    lax.fori_loop(0, tiles, gates, 0)
    for load in loads[PARTS + 4 :]:
        load.wait()
    of_all(x_send, x_recv, x_sems.at[0], x_sems.at[1], n - 1).wait()
    of_all(scale_recv, scale_recv, scale_sems.at[0], scale_sems.at[1], n - 1).wait()
    for h in range(2, PARTS):
        send_filter(h)

    unit = jnp.max(scale_recv[...], axis=0)
    scale_send[...] = unit

    def widen(i, _):
        at = pl.ds(pl.multiple_of(i * 8 * own, 8 * own), 8 * own)
        x = MIXED_CODE.decode(x_recv[pl.ds(i * 8, 8)]) * (scale_recv[pl.ds(i * 8, 8)] / unit)
        work[at, :] = x.reshape(8 * own, rows)
        return 0

    lax.fori_loop(0, n // 8, widen, 0)
    part_rows = blocks * part

    def over_rows(high, low, mat):
        return dot(high, mat[0]) + (dot(high, mat[1]) + dot(low, mat[0]))

    step_rows = min(256, part_rows)

    size = 2 * part
    for h in range(PARTS):

        def over_blocks(c, _, h=h):
            x = jnp.concatenate(
                [work[pl.ds(h * part + 2 * c + u, n, stride=own), :] for u in range(2)], axis=1
            )
            high, low = split(x)
            y = dot(outer_ref[...], jnp.concatenate((high, low, high), axis=0))
            cos, sin = tw_ref[0], tw_ref[1]
            for u in range(2):
                re, im = y[:blocks, u * rows : (u + 1) * rows], y[blocks:, u * rows : (u + 1) * rows]
                at = pl.ds(h * part_rows + 2 * c + u, blocks, stride=part)
                spec_re[at, :] = re * cos + im * sin
                spec_im[at, :] = im * cos - re * sin
            return 0

        for c in range(part // 2):
            over_blocks(c, 0)

        def forward(i, _, h=h):
            at = pl.ds(pl.multiple_of(h * part_rows + i * step_rows, step_rows), step_rows)
            high, low = split(jnp.concatenate((spec_re[at, :], spec_im[at, :]), axis=1))
            x = over_rows(high, low, fwd_ref)
            spec_re[at, :] = x[:, :rows]
            spec_im[at, :] = x[:, rows:]
            return 0

        lax.fori_loop(0, part_rows // step_rows, forward, 0)

        def backward(g, _, h=h):
            of_all(
                h_send.at[h], h_recv.at[h], h_send_sems.at[h], h_recv_sems.at[h, g], group
            ).wait_recv()

            def place(u):
                e = lax.rem(me - (g * group + u) + n, n)
                return e, pl.ds(pl.multiple_of(h * part_rows + e * size, size), size)

            for u in range(group):
                e, at = place(u)
                f = FILTER_CODE.decode(h_recv[h, e])
                f_re, f_im = f[:size], f[size:]
                re, im = spec_re[at, :], spec_im[at, :]
                high, low = split(jnp.concatenate((re * f_re - im * f_im, re * f_im + im * f_re), axis=1))
                stage_high[u * size : (u + 1) * size, :] = high
                stage_low[u * size : (u + 1) * size, :] = low
            x = over_rows(stage_high[...], stage_low[...], inv_ref)
            for u in range(group):
                _, at = place(u)
                spec_re[at, :] = x[u * size : (u + 1) * size, :rows]
                spec_im[at, :] = x[u * size : (u + 1) * size, rows:]
            return 0

        lax.fori_loop(0, GROUPS, backward, 0)

        def back_over_blocks(c, _, h=h):
            cos, sin = tw_ref[0], tw_ref[1]
            turned = []
            for u in range(2):
                at = pl.ds(h * part_rows + 2 * c + u, blocks, stride=part)
                re, im = spec_re[at, :], spec_im[at, :]
                turned.append(jnp.concatenate((re * cos - im * sin, im * cos + re * sin), axis=0))
            high, low = split(jnp.concatenate(turned, axis=1))
            y = dot(inner_ref[...], high)
            y = y[:n] + (y[n:] + dot(inner_ref[:n, :], low))
            for u in range(2):
                back[pl.ds(2 * c + u, n, stride=part), :] = y[:, u * rows : (u + 1) * rows]
            return 0

        for c in range(part // 2):
            back_over_blocks(c, 0)

        def narrow(i, _, h=h):
            at = pl.ds(pl.multiple_of(i * 8 * part, 8 * part), 8 * part)
            y_send[h, pl.ds(i * 8, 8)] = CONV_CODE.encode(back[at, :].reshape(8, part, rows))
            return 0

        for i in range(n // 8):
            narrow(i, 0)
        exchange(y_send.at[h], y_recv.at[h], y_sems.at[h])

    total = jnp.zeros((rows, 128), F32)
    for h in range(PARTS):
        of_all(y_send.at[h], y_recv.at[h], y_sems.at[h, 0], y_sems.at[h, 1], n - 1).wait()

        def gate(i, total, h=h):
            cols = pl.ds(pl.multiple_of(h * part_width + i * 128, 128), 128)
            conv = CONV_CODE.decode(y_recv[h, pl.ds(i * per_tile, per_tile)]).reshape(128, rows).T
            conv = conv * (bounds(cols) * scale_send[...])
            gated = query[:, cols] * (conv + skip_ref[:, cols] * mixed[:, cols])
            query[:, cols] = gated
            return total + gated * gated

        for i in range(tiles):
            total = gate(i, total)
    sums[0:1, :] = jnp.sum(total.T, axis=0, keepdims=True)
    sends = []
    for i in range(1, n_ch):
        copy = pltpu.make_async_remote_copy(
            src_ref=sums, dst_ref=sums_recv.at[i], send_sem=sum_send.at[i], recv_sem=sum_recv.at[i],
            device_id=(me, lax.rem(column + i, n_ch)), device_id_type=MESH,
        )
        copy.start()
        sends.append(copy)
    for h in range(PARTS):
        of_all(h_send.at[h], h_recv.at[h], h_send_sems.at[h], h_recv_sems.at[h, 0], n - 1).wait_send()
    query[...] = query[...] * gain_ref[...]
    square = sums[0:1, :]
    for i, copy in enumerate(sends):
        copy.wait()
        square = square + sums_recv[i + 1, 0:1, :]
    scale = lax.rsqrt(square / channels + EPS)
    scale = jnp.broadcast_to(scale, (128, rows)).T

    for i in range(PARTS * tiles):
        cols = pl.ds(i * 128, 128)
        out_ref[:, cols] = (query[:, cols] * scale).astype(BF16)


def per_device(q_in, k_in, v_in, short_taps, skip_bias, norm_gain, filter_spectrum):
    rows, width = q_in.shape
    n, n_ch = lax.axis_size("ctx"), lax.axis_size("ch")
    own = width // n
    part = own // PARTS
    blocks = 2 * n
    consts = tables(n, rows)
    anywhere = pl.BlockSpec(memory_space=pl.ANY)
    dma = pltpu.SemaphoreType.DMA
    like = [pltpu.VMEM(c.shape, c.dtype) for c in consts]
    return pl.pallas_call(
        functools.partial(kernel, n, n_ch, float(width * n_ch)),
        out_shape=pltpu.VMEM((rows, width), BF16),
        in_specs=[anywhere] * (7 + len(consts)),
        out_specs=pl.BlockSpec(memory_space=pltpu.VMEM),
        scratch_shapes=[
            pltpu.VMEM((3, rows, width), BF16),
            pltpu.VMEM(short_taps.shape, F32),
            pltpu.VMEM((1, width), F32),
            pltpu.VMEM((1, width), F32),
            pltpu.VMEM((PARTS, 4, rows, width // PARTS), F32),
            *like,
            pltpu.VMEM((3, rows + 8, width), F32),
            pltpu.VMEM((8, width), F32),
            pltpu.VMEM((8, width), F32),
            pltpu.VMEM((rows, width), F32),
            pltpu.VMEM((rows, width), F32),
            pltpu.VMEM((n, own, rows), BF16),
            pltpu.VMEM((n, own, rows), BF16),
            pltpu.VMEM((PARTS, n, 4 * part, rows), BF16),
            pltpu.VMEM((PARTS, n, 4 * part, rows), BF16),
            pltpu.VMEM((PARTS, n, part, rows), BF16),
            pltpu.VMEM((PARTS, n, part, rows), BF16),
            pltpu.VMEM((n * own, rows), F32),
            pltpu.VMEM((n * part, rows), F32),
            pltpu.VMEM((8, width), F32),
            pltpu.VMEM((1, 128), F32),
            pltpu.VMEM((n, 1, 128), F32),
            pltpu.VMEM((blocks * own, rows), F32),
            pltpu.VMEM((blocks * own, rows), F32),
            pltpu.VMEM((n // GROUPS * 2 * part, 2 * rows), BF16),
            pltpu.VMEM((n // GROUPS * 2 * part, 2 * rows), BF16),
            pltpu.VMEM((8, 128), F32),
            pltpu.VMEM((n_ch, 8, 128), F32),
            dma((11 + PARTS,)),
            dma((2,)),
            dma((2,)),
            dma((2,)),
            dma((PARTS,)),
            dma((PARTS, GROUPS)),
            dma((PARTS, 2)),
            dma((n_ch,)),
            dma((n_ch,)),
        ],
        compiler_params=pltpu.CompilerParams(
            collective_id=0, has_side_effects=True, vmem_limit_bytes=56 * 2**20
        ),
    )(
        q_in, k_in, v_in, short_taps, skip_bias[None], norm_gain[None],
        filter_spectrum.reshape(4, rows, width),
        *(jnp.asarray(c) for c in consts),
    )


def solution(mesh):
    placed = (
        P("ctx", "ch"),
        P("ctx", "ch"),
        P("ctx", "ch"),
        P(None, None, "ch"),
        P("ch"),
        P("ch"),
        P(None, "ctx", None, None, "ch"),
    )
    return jax.shard_map(
        per_device, mesh=mesh, in_specs=placed, out_specs=P("ctx", "ch"), check_vma=False
    )
```

```python
import functools

import jax
import jax.numpy as jnp
import numpy as np
from jax import lax
from jax.experimental import pallas as pl
from jax.experimental.pallas import tpu as pltpu
from jax.sharding import PartitionSpec as P

MESH = pl.DeviceIdType.MESH
F32 = jnp.float32
BF16 = jnp.bfloat16
EPS = 1e-06
BIAS = 125.0
LN2 = float(np.log(2.0))
IN_MAX = 6.0
PARTS = 4
GROUPS = 4


class Code:
    def __init__(self, power, top, knee=None, tail=1.0):
        self.power, self.top, self.tail = power, top, tail
        self.knee = top if knee is None else knee
        self.turn = 2.0 * BIAS - tail * float(np.log2(top / self.knee))
        self.a = (2.0 ** (self.turn / power) - 1.0) / self.knee

    def encode(self, x):
        size = jnp.minimum(jnp.abs(x), self.top)
        inner = jnp.minimum(size, self.knee)
        code = (self.power / LN2) * jnp.log(1.0 + self.a * inner) - BIAS
        if self.knee < self.top:
            code = code + (self.tail / LN2) * jnp.log(jnp.maximum(size * (1.0 / self.knee), 1.0))
        code = jnp.exp2(code)
        return jnp.where(x < 0.0, -code, code).astype(BF16)

    def decode(self, code):
        v = code.astype(F32)
        size = (1.0 / LN2) * jnp.log(jnp.abs(v)) + BIAS
        inner = jnp.minimum(size, self.turn) if self.knee < self.top else size
        x = (jnp.exp2((1.0 / self.power) * inner) - 1.0) * (1.0 / self.a)
        if self.knee < self.top:
            x = x * jnp.exp2((1.0 / self.tail) * (size - inner))
        return jnp.where(v < 0.0, -x, x)


FILTER_CODE = Code(30.0, 6.0)
MIXED_CODE = Code(24.0, 1.0)
CONV_CODE = Code(15.4, 768.0, 4.0, 4.0)


def split(x):
    high = x.astype(BF16)
    return high, (x - high.astype(F32)).astype(BF16)


def dot(a, b):
    return jnp.dot(a, b, preferred_element_type=F32)


def tables(devices, rows):
    levels = devices.bit_length() - 1
    rev = np.array([int(format(e, f"0{levels}b")[::-1], 2) if levels else 0 for e in range(devices)])
    freq = (2 * rev[:, None] + np.arange(2)[None, :]).reshape(-1)
    blocks = 2 * devices
    full = blocks * rows
    turn = 2.0 * np.pi
    ang = turn * ((freq[:, None] * np.arange(devices)[None, :]) % blocks) / blocks
    outer = np.concatenate((np.cos(ang), -np.sin(ang)), 0)
    tw = turn * ((freq[:, None] * np.arange(rows)[None, :]) % full) / full
    ids = np.arange(rows)
    loc = turn * ((ids[:, None] * ids[None, :]) % rows) / rows
    c, s = np.cos(loc), np.sin(loc)

    def parts(m):
        m = m.astype(np.float32)
        high = m.astype(jnp.bfloat16)
        return high, (m - high.astype(np.float32)).astype(jnp.bfloat16)

    outer_high, outer_low = parts(outer)
    return (
        np.concatenate((outer_high, outer_high, outer_low), 1),
        np.concatenate(parts(outer.T / full), 0),
        np.stack(parts(np.block([[c, -s], [s, c]]))),
        np.stack(parts(np.block([[c, s], [-s, c]]))),
        np.stack((np.cos(tw), np.sin(tw))).astype(np.float32),
    )


def kernel(
    n, n_ch, channels,
    q_hbm, k_hbm, v_hbm, taps_hbm, skip_hbm, gain_hbm, filt_hbm, *rest,
):
    consts_hbm, rest = rest[:5], rest[5:]
    (
        out_ref,
        feats, taps_ref, skip_ref, gain_ref, filt, outer_ref, inner_ref, fwd_ref, inv_ref, tw_ref,
        ext, halo_send, halo_recv, query, mixed, x_send, x_recv, h_send, h_recv, y_send, y_recv,
        work, back, peaks, scale_send, scale_recv, spec_re, spec_im, stage_high, stage_low, sums, sums_recv,
        in_sems, halo_sems, scale_sems, x_sems, h_send_sems, h_recv_sems, y_sems, sum_send, sum_recv,
    ) = rest
    me, column = lax.axis_index("ctx"), lax.axis_index("ch")
    rows, width = q_hbm.shape
    own = width // n
    part = own // PARTS
    part_width = width // PARTS
    tiles = part_width // 128
    per_tile = 128 // part
    blocks = 2 * n
    group = n // GROUPS
    ahead = lax.rem(me + 1, n)

    barrier = pltpu.get_barrier_semaphore()

    def greet(i, _):
        pl.semaphore_signal(barrier, inc=1, device_id=(lax.rem(me + i, n), column), device_id_type=MESH)
        return 0

    for i in range(1, n_ch):
        pl.semaphore_signal(barrier, inc=1, device_id=(me, lax.rem(column + i, n_ch)), device_id_type=MESH)
    lax.fori_loop(1, n, greet, 0)

    moves = [
        *((filt_hbm.at[:, :, pl.ds(h * part_width, part_width)], filt.at[h]) for h in range(PARTS)),
        (q_hbm, feats.at[0]),
        (k_hbm, feats.at[1]),
        (v_hbm, feats.at[2]),
        (taps_hbm, taps_ref),
        *zip(consts_hbm, (outer_ref, inner_ref, fwd_ref, inv_ref, tw_ref)),
        (skip_hbm, skip_ref),
        (gain_hbm, gain_ref),
    ]
    loads = [pltpu.make_async_copy(src, dst, in_sems.at[i]) for i, (src, dst) in enumerate(moves)]
    for load in loads:
        load.start()

    def code_filter(h):
        def step(i, _):
            cols = pl.ds(pl.multiple_of(i * 128, 128), 128)
            tiles_of = [
                FILTER_CODE.encode(filt[h, j, :, cols].T.reshape(per_tile, part, rows)) for j in range(4)
            ]
            h_send[h, pl.ds(i * per_tile, per_tile)] = jnp.concatenate(tiles_of, axis=1)
            return 0

        lax.fori_loop(0, tiles, step, 0)

    def send_filter(h):
        def step(i, _):
            to = lax.rem(me + i, n)
            pltpu.make_async_remote_copy(
                src_ref=h_send.at[h, to], dst_ref=h_recv.at[h, me],
                send_sem=h_send_sems.at[h], recv_sem=h_recv_sems.at[h, i // group],
                device_id=(to, column), device_id_type=MESH,
            ).start()
            return 0

        pltpu.make_async_copy(h_send.at[h, me], h_recv.at[h, me], h_recv_sems.at[h, 0]).start()
        lax.fori_loop(1, n, step, 0)

    def exchange(src, dst, sems):
        def step(i, _):
            to = lax.rem(me + i, n)
            pltpu.make_async_remote_copy(
                src_ref=src.at[to], dst_ref=dst.at[me], send_sem=sems.at[0], recv_sem=sems.at[1],
                device_id=(to, column), device_id_type=MESH,
            ).start()
            return 0

        lax.fori_loop(1, n, step, 0)
        dst[pl.ds(me, 1)] = src[pl.ds(me, 1)]

    def of_all(src, dst, send_sem, recv_sem, count):
        return pltpu.make_async_remote_copy(
            src_ref=src.at[pl.ds(0, count)], dst_ref=dst.at[pl.ds(0, count)], send_sem=send_sem, recv_sem=recv_sem,
            device_id=(ahead, column), device_id_type=MESH,
        )

    for load in loads[PARTS : PARTS + 3]:
        load.wait()
    for i in range(3):
        ext[i, 8 : 8 + rows, :] = feats[i].astype(F32)
        halo_send[2 * i : 2 * i + 2, :] = ext[i, 6 + rows : 8 + rows, :]
    halo_send[6:8, :] = jnp.zeros((2, width), F32)
    for i in (1, 2):
        peaks[i : i + 1, :] = jnp.max(jnp.abs(ext[i, 8 : 8 + rows, :]), axis=0, keepdims=True)
    sums[...] = jnp.zeros_like(sums)
    loads[0].wait()
    code_filter(0)
    pl.semaphore_wait(barrier, n - 1 + n_ch - 1)
    halo = pltpu.make_async_remote_copy(
        src_ref=halo_send, dst_ref=halo_recv, send_sem=halo_sems.at[0], recv_sem=halo_sems.at[1],
        device_id=(ahead, column), device_id_type=MESH,
    )
    halo.start()
    send_filter(0)
    loads[1].wait()
    code_filter(1)
    loads[PARTS + 3].wait()
    halo.wait()
    inside = jnp.where(me > 0, 1.0, 0.0)
    for i in range(3):
        ext[i, 6:8, :] = halo_recv[2 * i : 2 * i + 2, :] * inside

    highest = [
        jnp.max(jnp.maximum(peaks[i : i + 1, :], jnp.max(jnp.abs(ext[i, 6:8, :]), axis=0, keepdims=True)), axis=1, keepdims=True)
        for i in (1, 2)
    ]
    bound = jnp.maximum(highest[0] * highest[1] * (1.0 / IN_MAX**2), 1e-30)
    scale_send[...] = jnp.broadcast_to(bound, (1, 128))

    def bounds(cols):
        size = [sum(jnp.abs(taps_ref[i, lag : lag + 1, cols]) for lag in range(3)) * IN_MAX for i in (1, 2)]
        return jnp.maximum(size[0] * size[1], 1e-30)

    def short(which, cols):
        return sum(
            taps_ref[which, lag : lag + 1, cols] * ext[which, 8 - lag : 8 - lag + rows, cols] for lag in range(3)
        )

    def columns(h, i):
        return pl.ds(pl.multiple_of(h * part_width + i * 128, 128), 128)

    def mix(i, _):
        codes = []
        for h in range(PARTS):
            cols = columns(h, i)
            value = short(1, cols) * short(2, cols)
            mixed[:, cols] = value
            value = (value / bounds(cols)) * (1.0 / scale_send[...])
            codes.append(MIXED_CODE.encode(value.T.reshape(per_tile, part, rows)))
        x_send[pl.ds(i * per_tile, per_tile)] = jnp.concatenate(codes, axis=1)
        return 0

    lax.fori_loop(0, tiles, mix, 0)

    def send_bound(i, _):
        to = lax.rem(me + i, n)
        pltpu.make_async_remote_copy(
            src_ref=scale_send, dst_ref=scale_recv.at[me], send_sem=scale_sems.at[0], recv_sem=scale_sems.at[1],
            device_id=(to, column), device_id_type=MESH,
        ).start()
        return 0

    exchange(x_send, x_recv, x_sems)
    lax.fori_loop(1, n, send_bound, 0)
    scale_recv[pl.ds(me, 1)] = scale_send[...].reshape(1, 1, 128)
    send_filter(1)
    for h in range(2, PARTS):
        loads[h].wait()
        code_filter(h)

    def gates(i, _):
        for h in range(PARTS):
            cols = columns(h, i)
            query[:, cols] = short(0, cols)
        return 0

    lax.fori_loop(0, tiles, gates, 0)
    for load in loads[PARTS + 4 :]:
        load.wait()
    of_all(x_send, x_recv, x_sems.at[0], x_sems.at[1], n - 1).wait()
    of_all(scale_recv, scale_recv, scale_sems.at[0], scale_sems.at[1], n - 1).wait()
    for h in range(2, PARTS):
        send_filter(h)

    unit = jnp.max(scale_recv[...], axis=0)
    scale_send[...] = unit

    def widen(i, _):
        at = pl.ds(pl.multiple_of(i * 8 * own, 8 * own), 8 * own)
        x = MIXED_CODE.decode(x_recv[pl.ds(i * 8, 8)]) * (scale_recv[pl.ds(i * 8, 8)] / unit)
        work[at, :] = x.reshape(8 * own, rows)
        return 0

    lax.fori_loop(0, n // 8, widen, 0)
    part_rows = blocks * part

    def over_rows(high, low, mat):
        return dot(high, mat[0]) + (dot(high, mat[1]) + dot(low, mat[0]))

    step_rows = min(256, part_rows)

    size = 2 * part
    for h in range(PARTS):

        def over_blocks(c, _, h=h):
            x = jnp.concatenate(
                [work[pl.ds(h * part + 2 * c + u, n, stride=own), :] for u in range(2)], axis=1
            )
            high, low = split(x)
            y = dot(outer_ref[...], jnp.concatenate((high, low, high), axis=0))
            cos, sin = tw_ref[0], tw_ref[1]
            for u in range(2):
                re, im = y[:blocks, u * rows : (u + 1) * rows], y[blocks:, u * rows : (u + 1) * rows]
                at = pl.ds(h * part_rows + 2 * c + u, blocks, stride=part)
                spec_re[at, :] = re * cos + im * sin
                spec_im[at, :] = im * cos - re * sin
            return 0

        for c in range(part // 2):
            over_blocks(c, 0)

        def forward(i, _, h=h):
            at = pl.ds(pl.multiple_of(h * part_rows + i * step_rows, step_rows), step_rows)
            high, low = split(jnp.concatenate((spec_re[at, :], spec_im[at, :]), axis=1))
            x = over_rows(high, low, fwd_ref)
            spec_re[at, :] = x[:, :rows]
            spec_im[at, :] = x[:, rows:]
            return 0

        lax.fori_loop(0, part_rows // step_rows, forward, 0)

        def backward(g, _, h=h):
            of_all(
                h_send.at[h], h_recv.at[h], h_send_sems.at[h], h_recv_sems.at[h, g], group
            ).wait_recv()

            def place(u):
                e = lax.rem(me - (g * group + u) + n, n)
                return e, pl.ds(pl.multiple_of(h * part_rows + e * size, size), size)

            for u in range(group):
                e, at = place(u)
                f = FILTER_CODE.decode(h_recv[h, e])
                f_re, f_im = f[:size], f[size:]
                re, im = spec_re[at, :], spec_im[at, :]
                high, low = split(jnp.concatenate((re * f_re - im * f_im, re * f_im + im * f_re), axis=1))
                stage_high[u * size : (u + 1) * size, :] = high
                stage_low[u * size : (u + 1) * size, :] = low
            x = over_rows(stage_high[...], stage_low[...], inv_ref)
            for u in range(group):
                _, at = place(u)
                spec_re[at, :] = x[u * size : (u + 1) * size, :rows]
                spec_im[at, :] = x[u * size : (u + 1) * size, rows:]
            return 0

        lax.fori_loop(0, GROUPS, backward, 0)

        def back_over_blocks(c, _, h=h):
            cos, sin = tw_ref[0], tw_ref[1]
            turned = []
            for u in range(2):
                at = pl.ds(h * part_rows + 2 * c + u, blocks, stride=part)
                re, im = spec_re[at, :], spec_im[at, :]
                turned.append(jnp.concatenate((re * cos - im * sin, im * cos + re * sin), axis=0))
            high, low = split(jnp.concatenate(turned, axis=1))
            y = dot(inner_ref[...], high)
            y = y[:n] + (y[n:] + dot(inner_ref[:n, :], low))
            for u in range(2):
                back[pl.ds(2 * c + u, n, stride=part), :] = y[:, u * rows : (u + 1) * rows]
            return 0

        for c in range(part // 2):
            back_over_blocks(c, 0)

        def narrow(i, _, h=h):
            at = pl.ds(pl.multiple_of(i * 8 * part, 8 * part), 8 * part)
            y_send[h, pl.ds(i * 8, 8)] = CONV_CODE.encode(back[at, :].reshape(8, part, rows))
            return 0

        for i in range(n // 8):
            narrow(i, 0)
        exchange(y_send.at[h], y_recv.at[h], y_sems.at[h])

    total = jnp.zeros((rows, 128), F32)
    for h in range(PARTS):
        of_all(y_send.at[h], y_recv.at[h], y_sems.at[h, 0], y_sems.at[h, 1], n - 1).wait()

        def gate(i, total, h=h):
            cols = pl.ds(pl.multiple_of(h * part_width + i * 128, 128), 128)
            conv = CONV_CODE.decode(y_recv[h, pl.ds(i * per_tile, per_tile)]).reshape(128, rows).T
            conv = conv * (bounds(cols) * scale_send[...])
            gated = query[:, cols] * (conv + skip_ref[:, cols] * mixed[:, cols])
            query[:, cols] = gated
            return total + gated * gated

        for i in range(tiles):
            total = gate(i, total)
    sums[0:1, :] = jnp.sum(total.T, axis=0, keepdims=True)
    sends = []
    for i in range(1, n_ch):
        copy = pltpu.make_async_remote_copy(
            src_ref=sums, dst_ref=sums_recv.at[i], send_sem=sum_send.at[i], recv_sem=sum_recv.at[i],
            device_id=(me, lax.rem(column + i, n_ch)), device_id_type=MESH,
        )
        copy.start()
        sends.append(copy)
    for h in range(PARTS):
        of_all(h_send.at[h], h_recv.at[h], h_send_sems.at[h], h_recv_sems.at[h, 0], n - 1).wait_send()
    query[...] = query[...] * gain_ref[...]
    square = sums[0:1, :]
    for i, copy in enumerate(sends):
        copy.wait()
        square = square + sums_recv[i + 1, 0:1, :]
    scale = lax.rsqrt(square / channels + EPS)
    scale = jnp.broadcast_to(scale, (128, rows)).T

    for i in range(PARTS * tiles):
        cols = pl.ds(i * 128, 128)
        out_ref[:, cols] = (query[:, cols] * scale).astype(BF16)


def per_device(q_in, k_in, v_in, short_taps, skip_bias, norm_gain, filter_spectrum):
    rows, width = q_in.shape
    n, n_ch = lax.axis_size("ctx"), lax.axis_size("ch")
    own = width // n
    part = own // PARTS
    blocks = 2 * n
    consts = tables(n, rows)
    anywhere = pl.BlockSpec(memory_space=pl.ANY)
    dma = pltpu.SemaphoreType.DMA
    like = [pltpu.VMEM(c.shape, c.dtype) for c in consts]
    return pl.pallas_call(
        functools.partial(kernel, n, n_ch, float(width * n_ch)),
        out_shape=pltpu.VMEM((rows, width), BF16),
        in_specs=[anywhere] * (7 + len(consts)),
        out_specs=pl.BlockSpec(memory_space=pltpu.VMEM),
        scratch_shapes=[
            pltpu.VMEM((3, rows, width), BF16),
            pltpu.VMEM(short_taps.shape, F32),
            pltpu.VMEM((1, width), F32),
            pltpu.VMEM((1, width), F32),
            pltpu.VMEM((PARTS, 4, rows, width // PARTS), F32),
            *like,
            pltpu.VMEM((3, rows + 8, width), F32),
            pltpu.VMEM((8, width), F32),
            pltpu.VMEM((8, width), F32),
            pltpu.VMEM((rows, width), F32),
            pltpu.VMEM((rows, width), F32),
            pltpu.VMEM((n, own, rows), BF16),
            pltpu.VMEM((n, own, rows), BF16),
            pltpu.VMEM((PARTS, n, 4 * part, rows), BF16),
            pltpu.VMEM((PARTS, n, 4 * part, rows), BF16),
            pltpu.VMEM((PARTS, n, part, rows), BF16),
            pltpu.VMEM((PARTS, n, part, rows), BF16),
            pltpu.VMEM((n * own, rows), F32),
            pltpu.VMEM((n * part, rows), F32),
            pltpu.VMEM((8, width), F32),
            pltpu.VMEM((1, 128), F32),
            pltpu.VMEM((n, 1, 128), F32),
            pltpu.VMEM((blocks * own, rows), F32),
            pltpu.VMEM((blocks * own, rows), F32),
            pltpu.VMEM((n // GROUPS * 2 * part, 2 * rows), BF16),
            pltpu.VMEM((n // GROUPS * 2 * part, 2 * rows), BF16),
            pltpu.VMEM((8, 128), F32),
            pltpu.VMEM((n_ch, 8, 128), F32),
            dma((11 + PARTS,)),
            dma((2,)),
            dma((2,)),
            dma((2,)),
            dma((PARTS,)),
            dma((PARTS, GROUPS)),
            dma((PARTS, 2)),
            dma((n_ch,)),
            dma((n_ch,)),
        ],
        compiler_params=pltpu.CompilerParams(
            collective_id=0, has_side_effects=True, vmem_limit_bytes=56 * 2**20
        ),
    )(
        q_in, k_in, v_in, short_taps, skip_bias[None], norm_gain[None],
        filter_spectrum.reshape(4, rows, width),
        *(jnp.asarray(c) for c in consts),
    )


def solution(mesh):
    placed = (
        P("ctx", "ch"),
        P("ctx", "ch"),
        P("ctx", "ch"),
        P(None, None, "ch"),
        P("ch"),
        P("ch"),
        P(None, "ctx", None, None, "ch"),
    )
    return jax.shard_map(
        per_device, mesh=mesh, in_specs=placed, out_specs=P("ctx", "ch"), check_vma=False
    )
```

```python
import functools

import jax
import jax.numpy as jnp
import numpy as np
from jax import lax
from jax.experimental import pallas as pl
from jax.experimental.pallas import tpu as pltpu
from jax.sharding import PartitionSpec as P

MESH = pl.DeviceIdType.MESH
F32 = jnp.float32
BF16 = jnp.bfloat16
EPS = 1e-06
BIAS = 125.0
LN2 = float(np.log(2.0))
IN_MAX = 6.0
PARTS = 4
GROUPS = 2


class Code:
    def __init__(self, power, top, knee=None, tail=1.0):
        self.power, self.top, self.tail = power, top, tail
        self.knee = top if knee is None else knee
        self.turn = 2.0 * BIAS - tail * float(np.log2(top / self.knee))
        self.a = (2.0 ** (self.turn / power) - 1.0) / self.knee

    def encode(self, x):
        size = jnp.minimum(jnp.abs(x), self.top)
        inner = jnp.minimum(size, self.knee)
        code = (self.power / LN2) * jnp.log(1.0 + self.a * inner) - BIAS
        if self.knee < self.top:
            code = code + (self.tail / LN2) * jnp.log(jnp.maximum(size * (1.0 / self.knee), 1.0))
        code = jnp.exp2(code)
        return jnp.where(x < 0.0, -code, code).astype(BF16)

    def decode(self, code):
        v = code.astype(F32)
        size = (1.0 / LN2) * jnp.log(jnp.abs(v)) + BIAS
        inner = jnp.minimum(size, self.turn) if self.knee < self.top else size
        x = (jnp.exp2((1.0 / self.power) * inner) - 1.0) * (1.0 / self.a)
        if self.knee < self.top:
            x = x * jnp.exp2((1.0 / self.tail) * (size - inner))
        return jnp.where(v < 0.0, -x, x)


FILTER_CODE = Code(30.0, 6.0)
MIXED_CODE = Code(24.0, 1.0)
CONV_CODE = Code(15.4, 768.0, 4.0, 4.0)


def split(x):
    high = x.astype(BF16)
    return high, (x - high.astype(F32)).astype(BF16)


def dot(a, b):
    return jnp.dot(a, b, preferred_element_type=F32)


def tables(devices, rows):
    levels = devices.bit_length() - 1
    rev = np.array([int(format(e, f"0{levels}b")[::-1], 2) if levels else 0 for e in range(devices)])
    freq = (2 * rev[:, None] + np.arange(2)[None, :]).reshape(-1)
    blocks = 2 * devices
    full = blocks * rows
    turn = 2.0 * np.pi
    ang = turn * ((freq[:, None] * np.arange(devices)[None, :]) % blocks) / blocks
    outer = np.concatenate((np.cos(ang), -np.sin(ang)), 0)
    tw = turn * ((freq[:, None] * np.arange(rows)[None, :]) % full) / full
    ids = np.arange(rows)
    loc = turn * ((ids[:, None] * ids[None, :]) % rows) / rows
    c, s = np.cos(loc), np.sin(loc)

    def parts(m):
        m = m.astype(np.float32)
        high = m.astype(jnp.bfloat16)
        return high, (m - high.astype(np.float32)).astype(jnp.bfloat16)

    outer_high, outer_low = parts(outer)
    return (
        np.concatenate((outer_high, outer_high, outer_low), 1),
        np.concatenate(parts(outer.T / full), 0),
        np.stack(parts(np.block([[c, -s], [s, c]]))),
        np.stack(parts(np.block([[c, s], [-s, c]]))),
        np.stack((np.cos(tw), np.sin(tw))).astype(np.float32),
    )


def kernel(
    n, n_ch, channels,
    q_hbm, k_hbm, v_hbm, taps_hbm, skip_hbm, gain_hbm, filt_hbm, *rest,
):
    consts_hbm, rest = rest[:5], rest[5:]
    (
        out_ref,
        feats, taps_ref, skip_ref, gain_ref, filt, outer_ref, inner_ref, fwd_ref, inv_ref, tw_ref,
        ext, halo_send, halo_recv, query, mixed, x_send, x_recv, h_send, h_recv, y_send, y_recv,
        work, back, peaks, scale_send, scale_recv, spec_re, spec_im, stage_high, stage_low, sums, sums_recv,
        in_sems, halo_sems, scale_sems, x_sems, h_send_sems, h_recv_sems, y_sems, sum_send, sum_recv,
    ) = rest
    me, column = lax.axis_index("ctx"), lax.axis_index("ch")
    rows, width = q_hbm.shape
    own = width // n
    part = own // PARTS
    part_width = width // PARTS
    tiles = part_width // 128
    per_tile = 128 // part
    blocks = 2 * n
    group = n // GROUPS
    ahead = lax.rem(me + 1, n)

    barrier = pltpu.get_barrier_semaphore()

    def greet(i, _):
        pl.semaphore_signal(barrier, inc=1, device_id=(lax.rem(me + i, n), column), device_id_type=MESH)
        return 0

    for i in range(1, n_ch):
        pl.semaphore_signal(barrier, inc=1, device_id=(me, lax.rem(column + i, n_ch)), device_id_type=MESH)
    lax.fori_loop(1, n, greet, 0)

    moves = [
        *((filt_hbm.at[:, :, pl.ds(h * part_width, part_width)], filt.at[h]) for h in range(PARTS)),
        (q_hbm, feats.at[0]),
        (k_hbm, feats.at[1]),
        (v_hbm, feats.at[2]),
        (taps_hbm, taps_ref),
        *zip(consts_hbm, (outer_ref, inner_ref, fwd_ref, inv_ref, tw_ref)),
        (skip_hbm, skip_ref),
        (gain_hbm, gain_ref),
    ]
    loads = [pltpu.make_async_copy(src, dst, in_sems.at[i]) for i, (src, dst) in enumerate(moves)]
    for load in loads:
        load.start()

    def code_filter(h):
        def step(i, _):
            cols = pl.ds(pl.multiple_of(i * 128, 128), 128)
            tiles_of = [
                FILTER_CODE.encode(filt[h, j, :, cols].T.reshape(per_tile, part, rows)) for j in range(4)
            ]
            h_send[h, pl.ds(i * per_tile, per_tile)] = jnp.concatenate(tiles_of, axis=1)
            return 0

        lax.fori_loop(0, tiles, step, 0)

    def send_filter(h):
        def step(i, _):
            to = lax.rem(me + i, n)
            pltpu.make_async_remote_copy(
                src_ref=h_send.at[h, to], dst_ref=h_recv.at[h, me],
                send_sem=h_send_sems.at[h], recv_sem=h_recv_sems.at[h, i // group],
                device_id=(to, column), device_id_type=MESH,
            ).start()
            return 0

        pltpu.make_async_copy(h_send.at[h, me], h_recv.at[h, me], h_recv_sems.at[h, 0]).start()
        lax.fori_loop(1, n, step, 0)

    def exchange(src, dst, sems):
        def step(i, _):
            to = lax.rem(me + i, n)
            pltpu.make_async_remote_copy(
                src_ref=src.at[to], dst_ref=dst.at[me], send_sem=sems.at[0], recv_sem=sems.at[1],
                device_id=(to, column), device_id_type=MESH,
            ).start()
            return 0

        lax.fori_loop(1, n, step, 0)
        dst[pl.ds(me, 1)] = src[pl.ds(me, 1)]

    def of_all(src, dst, send_sem, recv_sem, count):
        return pltpu.make_async_remote_copy(
            src_ref=src.at[pl.ds(0, count)], dst_ref=dst.at[pl.ds(0, count)], send_sem=send_sem, recv_sem=recv_sem,
            device_id=(ahead, column), device_id_type=MESH,
        )

    for load in loads[PARTS : PARTS + 3]:
        load.wait()
    for i in range(3):
        ext[i, 8 : 8 + rows, :] = feats[i].astype(F32)
        halo_send[2 * i : 2 * i + 2, :] = ext[i, 6 + rows : 8 + rows, :]
    halo_send[6:8, :] = jnp.zeros((2, width), F32)
    for i in (1, 2):
        peaks[i : i + 1, :] = jnp.max(jnp.abs(ext[i, 8 : 8 + rows, :]), axis=0, keepdims=True)
    sums[...] = jnp.zeros_like(sums)
    loads[0].wait()
    code_filter(0)
    pl.semaphore_wait(barrier, n - 1 + n_ch - 1)
    halo = pltpu.make_async_remote_copy(
        src_ref=halo_send, dst_ref=halo_recv, send_sem=halo_sems.at[0], recv_sem=halo_sems.at[1],
        device_id=(ahead, column), device_id_type=MESH,
    )
    halo.start()
    send_filter(0)
    loads[1].wait()
    code_filter(1)
    loads[PARTS + 3].wait()
    halo.wait()
    inside = jnp.where(me > 0, 1.0, 0.0)
    for i in range(3):
        ext[i, 6:8, :] = halo_recv[2 * i : 2 * i + 2, :] * inside

    highest = [
        jnp.max(jnp.maximum(peaks[i : i + 1, :], jnp.max(jnp.abs(ext[i, 6:8, :]), axis=0, keepdims=True)), axis=1, keepdims=True)
        for i in (1, 2)
    ]
    bound = jnp.maximum(highest[0] * highest[1] * (1.0 / IN_MAX**2), 1e-30)
    scale_send[...] = jnp.broadcast_to(bound, (1, 128))

    def bounds(cols):
        size = [sum(jnp.abs(taps_ref[i, lag : lag + 1, cols]) for lag in range(3)) * IN_MAX for i in (1, 2)]
        return jnp.maximum(size[0] * size[1], 1e-30)

    def short(which, cols):
        return sum(
            taps_ref[which, lag : lag + 1, cols] * ext[which, 8 - lag : 8 - lag + rows, cols] for lag in range(3)
        )

    def columns(h, i):
        return pl.ds(pl.multiple_of(h * part_width + i * 128, 128), 128)

    def mix(i, _):
        codes = []
        for h in range(PARTS):
            cols = columns(h, i)
            value = short(1, cols) * short(2, cols)
            mixed[:, cols] = value
            value = (value / bounds(cols)) * (1.0 / scale_send[...])
            codes.append(MIXED_CODE.encode(value.T.reshape(per_tile, part, rows)))
        x_send[pl.ds(i * per_tile, per_tile)] = jnp.concatenate(codes, axis=1)
        return 0

    lax.fori_loop(0, tiles, mix, 0)

    def send_mixed(i, _):
        to = lax.rem(me + i, n)
        for src, dst, sems in ((scale_send, scale_recv, scale_sems), (x_send.at[to], x_recv, x_sems)):
            pltpu.make_async_remote_copy(
                src_ref=src, dst_ref=dst.at[me], send_sem=sems.at[0], recv_sem=sems.at[1],
                device_id=(to, column), device_id_type=MESH,
            ).start()
        return 0

    lax.fori_loop(1, n, send_mixed, 0)
    x_recv[pl.ds(me, 1)] = x_send[pl.ds(me, 1)]
    scale_recv[pl.ds(me, 1)] = scale_send[...].reshape(1, 1, 128)
    send_filter(1)
    for h in range(2, PARTS):
        loads[h].wait()
        code_filter(h)

    def gates(i, _):
        for h in range(PARTS):
            cols = columns(h, i)
            query[:, cols] = short(0, cols)
        return 0

    lax.fori_loop(0, tiles, gates, 0)
    for load in loads[PARTS + 4 :]:
        load.wait()
    of_all(x_send, x_recv, x_sems.at[0], x_sems.at[1], n - 1).wait()
    of_all(scale_recv, scale_recv, scale_sems.at[0], scale_sems.at[1], n - 1).wait()
    for h in range(2, PARTS):
        send_filter(h)

    unit = jnp.max(scale_recv[...], axis=0)
    scale_send[...] = unit

    def widen(i, _):
        at = pl.ds(pl.multiple_of(i * 8 * own, 8 * own), 8 * own)
        x = MIXED_CODE.decode(x_recv[pl.ds(i * 8, 8)]) * (scale_recv[pl.ds(i * 8, 8)] / unit)
        work[at, :] = x.reshape(8 * own, rows)
        return 0

    lax.fori_loop(0, n // 8, widen, 0)
    part_rows = blocks * part

    def over_rows(high, low, mat):
        return dot(high, mat[0]) + (dot(high, mat[1]) + dot(low, mat[0]))

    step_rows = min(256, part_rows)

    size = 2 * part
    for h in range(PARTS):

        def over_blocks(c, _, h=h):
            x = jnp.concatenate(
                [work[pl.ds(h * part + 2 * c + u, n, stride=own), :] for u in range(2)], axis=1
            )
            high, low = split(x)
            y = dot(outer_ref[...], jnp.concatenate((high, low, high), axis=0))
            cos, sin = tw_ref[0], tw_ref[1]
            for u in range(2):
                re, im = y[:blocks, u * rows : (u + 1) * rows], y[blocks:, u * rows : (u + 1) * rows]
                at = pl.ds(h * part_rows + 2 * c + u, blocks, stride=part)
                spec_re[at, :] = re * cos + im * sin
                spec_im[at, :] = im * cos - re * sin
            return 0

        for c in range(part // 2):
            over_blocks(c, 0)

        def forward(i, _, h=h):
            at = pl.ds(pl.multiple_of(h * part_rows + i * step_rows, step_rows), step_rows)
            high, low = split(jnp.concatenate((spec_re[at, :], spec_im[at, :]), axis=1))
            x = over_rows(high, low, fwd_ref)
            spec_re[at, :] = x[:, :rows]
            spec_im[at, :] = x[:, rows:]
            return 0

        lax.fori_loop(0, part_rows // step_rows, forward, 0)

        def backward(g, _, h=h):
            of_all(
                h_send.at[h], h_recv.at[h], h_send_sems.at[h], h_recv_sems.at[h, g], group
            ).wait_recv()

            def place(u):
                e = lax.rem(me - (g * group + u) + n, n)
                return e, pl.ds(pl.multiple_of(h * part_rows + e * size, size), size)

            for u in range(group):
                e, at = place(u)
                f = FILTER_CODE.decode(h_recv[h, e])
                f_re, f_im = f[:size], f[size:]
                re, im = spec_re[at, :], spec_im[at, :]
                high, low = split(jnp.concatenate((re * f_re - im * f_im, re * f_im + im * f_re), axis=1))
                stage_high[u * size : (u + 1) * size, :] = high
                stage_low[u * size : (u + 1) * size, :] = low
            x = over_rows(stage_high[...], stage_low[...], inv_ref)
            for u in range(group):
                _, at = place(u)
                spec_re[at, :] = x[u * size : (u + 1) * size, :rows]
                spec_im[at, :] = x[u * size : (u + 1) * size, rows:]
            return 0

        lax.fori_loop(0, GROUPS, backward, 0)

        def back_over_blocks(c, _, h=h):
            cos, sin = tw_ref[0], tw_ref[1]
            turned = []
            for u in range(2):
                at = pl.ds(h * part_rows + 2 * c + u, blocks, stride=part)
                re, im = spec_re[at, :], spec_im[at, :]
                turned.append(jnp.concatenate((re * cos - im * sin, im * cos + re * sin), axis=0))
            high, low = split(jnp.concatenate(turned, axis=1))
            y = dot(inner_ref[...], high)
            y = y[:n] + (y[n:] + dot(inner_ref[:n, :], low))
            for u in range(2):
                back[pl.ds(2 * c + u, n, stride=part), :] = y[:, u * rows : (u + 1) * rows]
            return 0

        for c in range(part // 2):
            back_over_blocks(c, 0)

        def narrow(i, _, h=h):
            at = pl.ds(pl.multiple_of(i * 8 * part, 8 * part), 8 * part)
            y_send[h, pl.ds(i * 8, 8)] = CONV_CODE.encode(back[at, :].reshape(8, part, rows))
            return 0

        for i in range(n // 8):
            narrow(i, 0)
        exchange(y_send.at[h], y_recv.at[h], y_sems.at[h])

    total = jnp.zeros((rows, 128), F32)
    for h in range(PARTS):
        of_all(y_send.at[h], y_recv.at[h], y_sems.at[h, 0], y_sems.at[h, 1], n - 1).wait()

        def gate(i, total, h=h):
            cols = pl.ds(pl.multiple_of(h * part_width + i * 128, 128), 128)
            conv = CONV_CODE.decode(y_recv[h, pl.ds(i * per_tile, per_tile)]).reshape(128, rows).T
            conv = conv * (bounds(cols) * scale_send[...])
            gated = query[:, cols] * (conv + skip_ref[:, cols] * mixed[:, cols])
            query[:, cols] = gated
            return total + gated * gated

        for i in range(tiles):
            total = gate(i, total)
    sums[0:1, :] = jnp.sum(total.T, axis=0, keepdims=True)
    sends = []
    for i in range(1, n_ch):
        copy = pltpu.make_async_remote_copy(
            src_ref=sums, dst_ref=sums_recv.at[i], send_sem=sum_send.at[i], recv_sem=sum_recv.at[i],
            device_id=(me, lax.rem(column + i, n_ch)), device_id_type=MESH,
        )
        copy.start()
        sends.append(copy)
    for h in range(PARTS):
        of_all(h_send.at[h], h_recv.at[h], h_send_sems.at[h], h_recv_sems.at[h, 0], n - 1).wait_send()
    query[...] = query[...] * gain_ref[...]
    square = sums[0:1, :]
    for i, copy in enumerate(sends):
        copy.wait()
        square = square + sums_recv[i + 1, 0:1, :]
    scale = lax.rsqrt(square / channels + EPS)
    scale = jnp.broadcast_to(scale, (128, rows)).T

    for i in range(PARTS * tiles):
        cols = pl.ds(i * 128, 128)
        out_ref[:, cols] = (query[:, cols] * scale).astype(BF16)


def per_device(q_in, k_in, v_in, short_taps, skip_bias, norm_gain, filter_spectrum):
    rows, width = q_in.shape
    n, n_ch = lax.axis_size("ctx"), lax.axis_size("ch")
    own = width // n
    part = own // PARTS
    blocks = 2 * n
    consts = tables(n, rows)
    anywhere = pl.BlockSpec(memory_space=pl.ANY)
    dma = pltpu.SemaphoreType.DMA
    like = [pltpu.VMEM(c.shape, c.dtype) for c in consts]
    return pl.pallas_call(
        functools.partial(kernel, n, n_ch, float(width * n_ch)),
        out_shape=pltpu.VMEM((rows, width), BF16),
        in_specs=[anywhere] * (7 + len(consts)),
        out_specs=pl.BlockSpec(memory_space=pltpu.VMEM),
        scratch_shapes=[
            pltpu.VMEM((3, rows, width), BF16),
            pltpu.VMEM(short_taps.shape, F32),
            pltpu.VMEM((1, width), F32),
            pltpu.VMEM((1, width), F32),
            pltpu.VMEM((PARTS, 4, rows, width // PARTS), F32),
            *like,
            pltpu.VMEM((3, rows + 8, width), F32),
            pltpu.VMEM((8, width), F32),
            pltpu.VMEM((8, width), F32),
            pltpu.VMEM((rows, width), F32),
            pltpu.VMEM((rows, width), F32),
            pltpu.VMEM((n, own, rows), BF16),
            pltpu.VMEM((n, own, rows), BF16),
            pltpu.VMEM((PARTS, n, 4 * part, rows), BF16),
            pltpu.VMEM((PARTS, n, 4 * part, rows), BF16),
            pltpu.VMEM((PARTS, n, part, rows), BF16),
            pltpu.VMEM((PARTS, n, part, rows), BF16),
            pltpu.VMEM((n * own, rows), F32),
            pltpu.VMEM((n * part, rows), F32),
            pltpu.VMEM((8, width), F32),
            pltpu.VMEM((1, 128), F32),
            pltpu.VMEM((n, 1, 128), F32),
            pltpu.VMEM((blocks * own, rows), F32),
            pltpu.VMEM((blocks * own, rows), F32),
            pltpu.VMEM((n // GROUPS * 2 * part, 2 * rows), BF16),
            pltpu.VMEM((n // GROUPS * 2 * part, 2 * rows), BF16),
            pltpu.VMEM((8, 128), F32),
            pltpu.VMEM((n_ch, 8, 128), F32),
            dma((11 + PARTS,)),
            dma((2,)),
            dma((2,)),
            dma((2,)),
            dma((PARTS,)),
            dma((PARTS, GROUPS)),
            dma((PARTS, 2)),
            dma((n_ch,)),
            dma((n_ch,)),
        ],
        compiler_params=pltpu.CompilerParams(
            collective_id=0, has_side_effects=True, vmem_limit_bytes=56 * 2**20
        ),
    )(
        q_in, k_in, v_in, short_taps, skip_bias[None], norm_gain[None],
        filter_spectrum.reshape(4, rows, width),
        *(jnp.asarray(c) for c in consts),
    )


def solution(mesh):
    placed = (
        P("ctx", "ch"),
        P("ctx", "ch"),
        P("ctx", "ch"),
        P(None, None, "ch"),
        P("ch"),
        P("ch"),
        P(None, "ctx", None, None, "ch"),
    )
    return jax.shard_map(
        per_device, mesh=mesh, in_specs=placed, out_specs=P("ctx", "ch"), check_vma=False
    )
```
